128 devices in a mesh: dp: 32 (over z, y, core), feat: 4 (over x).
Axes of the slice: x: 4, y: 4, z: 4, core: 2. Of those that a mesh axis runs over, the one named last changes fastest.
Arguments:
- features: bfloat16 [131072, 8192], P('dp', 'feat'), may hold values from -6 to 6
- fixed_weight: float32 [8192], P('feat'), may hold values from -0.0625 to 0.0625
- prior_offset: float32 [131072], P('dp'), may hold values from -6 to 6
- labels: int32 [131072], P('dp'), may hold values 0 or 1
- impression_member: int32 [131072], P(('dp', 'feat')), may hold values from 0 to 4095, as said below
- member_position: int32 [4096], replicated, may hold values from 0 to 4095, as said below
- member_counts: int32 [4096], P(('dp', 'feat')), may hold values from 0 to 128, as said below
- member_features: float32 [131072, 256], P(('dp', 'feat')), may hold values from -6 to 6
- member_params: float32 [4096, 256], P(('dp', 'feat')), may hold values from -0.375 to 0.375
Outputs:
- updated_weight: float32 [8192], P('feat')
- updated_params: float32 [4096, 256], P(('dp', 'feat'))
- total_margin: float32 [131072], P(('dp', 'feat'))
The draws below stay inside these ranges and needn't reach their ends.
Inputs may be any that keep to these rules, and one draw needn't show every extreme that they name: `impression_member`: among the 1024 rows of one device, at most 16 name members whose position lies with any one owner (owner = member_position[id] // 32, devices in dp+feat order), and at most 1 names any one member; in every draw one owner receives exactly 16 rows from every device. `member_position`: A permutation of the positions; position p is row p % 32 of device p // 32 of dp+feat. `member_counts`: the number of examples whose member sits at each position.
All inputs are finite; a program needn't handle non-finite values. No bound on the sum of `labels` on one device may be relied on, other than what follows from the above.
Results may differ from the reference program's by a relative error of at most 0.0026.
Values sent between devices are 32-bit elements; how exact they have to be, the bound alone decides.
No kernel may reach another device: no remote copies, remote signals or barrier semaphores. Data moves between devices by JAX's collectives and lax.ppermute only.
A program may use at most 128 MiB of HBM per device.

```python
import jax
import jax.numpy as jnp
from jax import lax

FEATURES = 8192
MEMBER_WIDTH = 256
CG_STEPS = 3
MEM_DEV = 32
ROW_DEV = 1024
OWNERS = 128
CAPACITY = 16
MEMBERS = 4096
EXAMPLES = 131072


def member_layout(key):
    member_position = jax.random.permutation(jax.random.fold_in(key, 11), MEMBERS).astype(jnp.int32)
    busiest = jax.random.randint(jax.random.fold_in(key, 12), (), 0, OWNERS).astype(jnp.int32)
    owner_range = jnp.arange(OWNERS, dtype=jnp.int32)

    def one_source(source_key):
        ordering = jax.random.permutation(source_key, (OWNERS - 1) * CAPACITY).astype(jnp.int32)
        picked = ordering[:ROW_DEV - CAPACITY] // CAPACITY
        others = picked + (picked >= busiest).astype(jnp.int32)
        owners = jnp.concatenate([jnp.zeros((CAPACITY,), jnp.int32) + busiest, others])
        owners = jax.random.permutation(jax.random.fold_in(source_key, 1), owners)
        owner_hot = (owners[:, None] == owner_range[None, :]).astype(jnp.int32)
        group_rank = jnp.sum(jnp.cumsum(owner_hot, axis=0) * owner_hot, axis=1) - 1
        shifts = jax.random.randint(jax.random.fold_in(source_key, 2), (OWNERS,), 0, MEM_DEV).astype(jnp.int32)
        shifts = jnp.where(owner_range == busiest, 0, shifts)
        slot_ids = (group_rank + shifts[owners]) % MEM_DEV
        return owners * MEM_DEV + slot_ids
    source_keys = jax.random.split(jax.random.fold_in(key, 13), OWNERS)
    positions = jax.vmap(one_source)(source_keys).reshape(-1)
    return (member_position, positions)


def draw_impression_member(key, part):
    member_position, positions = member_layout(key)
    inverse = jnp.zeros((MEMBERS,), jnp.int32).at[member_position].set(jnp.arange(MEMBERS, dtype=jnp.int32))
    return inverse[positions]


def draw_member_position(key, part):
    member_position, positions = member_layout(key)
    return member_position


def draw_member_counts(key, part):
    member_position, positions = member_layout(key)
    return jnp.zeros((MEMBERS,), jnp.int32).at[positions].add(1)


def touch_ends(drawn, key, least, top_value):
    longest = drawn.shape.index(max(drawn.shape))
    spots = []
    for shift in (0, 1):
        where = [jax.random.randint(jax.random.fold_in(key, axis), (), 0, length) for axis, length in enumerate(drawn.shape)]
        where[longest] = (where[longest] + shift) % drawn.shape[longest]
        spots.append(tuple(where))
    return drawn.at[spots[0]].set(least).at[spots[1]].set(top_value)


def level_of(key, shape, cuts, smallest, top_value):
    loudness, own = 1.0, jax.random.fold_in(key, 6)
    for position, blocks in cuts:
        steps = jnp.exp(jax.random.uniform(jax.random.fold_in(own, position), (blocks,), jnp.float32, smallest / len(cuts), top_value / len(cuts)))
        loudness = loudness * jnp.repeat(steps, shape[position] // blocks).reshape([-1 if axis == position else 1 for axis in range(len(shape))])
    return loudness


def scatter_about(own_key, dims, width, most, shards=(), kind=jnp.bfloat16):
    factor_of = level_of(own_key, dims, shards, -0.22, 0.18) if shards else 1.0
    drawn = jax.random.normal(own_key, dims, jnp.float32) * width * factor_of
    return jnp.minimum(jnp.maximum(drawn, -most), most).astype(kind)


def setup_inputs(seed: int = 0) -> dict:
    streams_of = jax.random.split(jax.random.key(seed), 10)
    features = scatter_about(streams_of[0], (EXAMPLES, FEATURES), 1.0, 6.0, ((0, 32), (1, 4)))
    fixed_weight = scatter_about(streams_of[1], (FEATURES,), FEATURES ** -0.5, 0.0625, ((0, 4),), jnp.float32)
    prior_offset = scatter_about(streams_of[2], (EXAMPLES,), 1.0, 6.0, ((0, 32),), jnp.float32)
    labels = touch_ends((jax.random.randint(streams_of[3], (EXAMPLES,), 0, 2) < 1).astype(jnp.int32), jax.random.fold_in(streams_of[3], 1), 0, 1)
    impression_member = draw_impression_member(jax.random.fold_in(streams_of[9], 71), 0)
    member_position = draw_member_position(jax.random.fold_in(streams_of[9], 71), 0)
    member_counts = draw_member_counts(jax.random.fold_in(streams_of[9], 71), 0)
    member_features = scatter_about(streams_of[7], (EXAMPLES, MEMBER_WIDTH), 1.0, 6.0, ((0, 128),), jnp.float32)
    member_params = scatter_about(streams_of[8], (MEMBERS, MEMBER_WIDTH), MEMBER_WIDTH ** -0.5, 0.375, ((0, 128),), jnp.float32)
    return {"features": features, "fixed_weight": fixed_weight, "prior_offset": prior_offset, "labels": labels, "impression_member": impression_member, "member_position": member_position, "member_counts": member_counts, "member_features": member_features, "member_params": member_params}


ridge_fixed = 0.1
step_fixed = 2.0
ridge_member = 0.25
tiny_add = 1e-30
highest = lax.Precision.HIGHEST


def reference(features, fixed_weight, prior_offset, labels, impression_member, member_position, member_counts, member_features, member_params):
    label_all = labels.astype(jnp.float32)
    margin_old = jnp.dot(features, fixed_weight.astype(jnp.bfloat16), preferred_element_type=jnp.float32) + prior_offset
    residual = (jax.nn.sigmoid(margin_old) - label_all).astype(jnp.bfloat16)
    gradient = jnp.dot(residual, features, preferred_element_type=jnp.float32) / EXAMPLES + ridge_fixed * fixed_weight
    updated_weight = fixed_weight - step_fixed * gradient
    fixed_new = jnp.dot(features, updated_weight.astype(jnp.bfloat16), preferred_element_type=jnp.float32)
    positions = member_position[impression_member].astype(jnp.int32)
    old_score = jnp.sum(member_features * member_params[positions], axis=1)
    probability = jax.nn.sigmoid(fixed_new + old_score)
    weights = probability * (1.0 - probability)
    errors = label_all - probability
    scaling = 1.0 / (member_counts.astype(jnp.float32) + 1.0)
    rhs_vec = jax.ops.segment_sum(member_features * errors[:, None], positions, num_segments=MEMBERS) * scaling[:, None] - ridge_member * member_params

    def add_block(running, number):
        offset_row = number * ROW_DEV
        row_block = lax.dynamic_slice_in_dim(member_features, offset_row, ROW_DEV, 0)
        weight_block = lax.dynamic_slice_in_dim(weights, offset_row, ROW_DEV, 0)
        position_block = lax.dynamic_slice_in_dim(positions, offset_row, ROW_DEV, 0)
        outer_sum = (row_block * weight_block[:, None])[:, :, None] * row_block[:, None, :]
        return running.at[position_block].add(outer_sum), None

    gram_all, _ = lax.scan(add_block, jnp.zeros((MEMBERS, MEMBER_WIDTH, MEMBER_WIDTH), jnp.float32), jnp.arange(EXAMPLES // ROW_DEV, dtype=jnp.int32))
    system = gram_all * scaling[:, None, None] + ridge_member * jnp.eye(MEMBER_WIDTH, dtype=jnp.float32)
    solution = jnp.zeros_like(rhs_vec)
    remains = rhs_vec
    direction = rhs_vec
    norm_now = jnp.sum(remains * remains, axis=1)
    for _ in range(CG_STEPS):
        images = jnp.einsum("mkl,ml->mk", system, direction, precision=highest)
        step_size = norm_now / (jnp.sum(direction * images, axis=1) + tiny_add)
        solution = solution + step_size[:, None] * direction
        remains = remains - step_size[:, None] * images
        norm_next = jnp.sum(remains * remains, axis=1)
        direction = remains + (norm_next / (norm_now + tiny_add))[:, None] * direction
        norm_now = norm_next
    updated_params = member_params + solution
    new_score = jnp.sum(member_features * updated_params[positions], axis=1)
    return updated_weight, updated_params, fixed_new + new_score
```

```python
import functools

import jax
import jax.numpy as jnp
from jax import lax
from jax.experimental import pallas as pl
from jax.experimental.pallas import tpu as pltpu
from jax.sharding import Mesh
from jax.sharding import PartitionSpec as P

RIDGE_FIXED = 0.1
STEP_FIXED = 2.0
RIDGE_MEMBER = 0.25
TINY = 1e-30
CG_STEPS = 3
F32 = jnp.float32
BF16 = jnp.bfloat16
LANES = 128
CAPACITY = 16
ALL = ("z", "y", "core", "feat")
NN = (((1,), (0,)), ((), ()))
NT = (((1,), (1,)), ((), ()))
TN = (((0,), (0,)), ((), ()))
VMEM_SPEC = pl.BlockSpec(memory_space=pltpu.VMEM)


def dot(left, right, dims):
    return lax.dot_general(left, right, dims, preferred_element_type=F32)


def split(value):
    high = value.astype(BF16)
    return high, (value - high.astype(F32)).astype(BF16)


def dot_split(left, high, low, dims):
    left_high, left_low = split(left)
    rows = left.shape[0]
    both = dot(jnp.concatenate([left_high, left_low], axis=0), high, dims)
    return both[:rows] + both[rows:] + dot(left_high, low, dims)


def sublane_iota(shape):
    return lax.broadcasted_iota(jnp.int32, shape, 0)


def lane_iota(shape):
    return lax.broadcasted_iota(jnp.int32, shape, 1)


def hot_rows(count, index):
    shape = (count, index.shape[1])
    return jnp.where(sublane_iota(shape) == index, 1.0, 0.0).astype(BF16)


def params(vmem_mib):
    return pltpu.CompilerParams(vmem_limit_bytes=vmem_mib << 20)


def route_kernel(ids_ref, table_ref, labels_ref, rows_ref, target_ref, buf_ref, meta_ref, *, mem_dev):
    rows = ids_ref.shape[1]
    ids = ids_ref[...]
    table = table_ref[...]
    owner_table = (table // mem_dev).astype(F32).astype(BF16)
    slot_table = (table % mem_dev).astype(F32).astype(BF16)
    both = jnp.concatenate([owner_table, slot_table], axis=1)
    found = dot(both, hot_rows(table.shape[0], ids // LANES), TN)
    low_hot = sublane_iota((LANES, rows)) == ids % LANES
    owner = jnp.sum(jnp.where(low_hot, found[:LANES], 0.0), axis=0, keepdims=True)
    slot = jnp.sum(jnp.where(low_hot, found[LANES:], 0.0), axis=0, keepdims=True)
    owner_hot = sublane_iota((LANES, rows)) == owner.astype(jnp.int32)
    hot = jnp.where(owner_hot, 1.0, 0.0).astype(BF16)
    earlier = jnp.where(sublane_iota((rows, rows)) < lane_iota((rows, rows)), 1.0, 0.0).astype(BF16)
    before = dot(hot, earlier, NN)
    rank = jnp.sum(jnp.where(owner_hot, before, 0.0), axis=0, keepdims=True).astype(jnp.int32)
    target = owner.astype(jnp.int32) * CAPACITY + rank
    target_ref[...] = target
    slot_hot = jnp.where(owner_hot, slot, 0.0).astype(BF16)
    label_hot = jnp.where(owner_hot, labels_ref[...].astype(F32), 0.0).astype(BF16)
    meta_ref[...] = dot(slot_hot, hot_rows(LANES, rank + 4 * CAPACITY), NT) + dot(
        label_hot, hot_rows(LANES, rank + 5 * CAPACITY), NT
    )
    high, low = split(rows_ref[...])
    parts = jnp.concatenate([high, low], axis=1)
    width = rows_ref.shape[1]
    step = 256
    for start in range(0, buf_ref.shape[0], step):
        place = jnp.where(sublane_iota((step, rows)) + start == target, 1.0, 0.0).astype(BF16)
        moved = dot(place, parts, NN)
        buf_ref[start : start + step, :] = moved[:, :width] + moved[:, width:]


def route(ids, table, labels, rows, mem_dev):
    count = ids.shape[1]
    slots = LANES * CAPACITY
    return pl.pallas_call(
        functools.partial(route_kernel, mem_dev=mem_dev),
        in_specs=[VMEM_SPEC] * 4,
        out_specs=[VMEM_SPEC] * 3,
        out_shape=[
            jax.ShapeDtypeStruct((1, count), jnp.int32),
            jax.ShapeDtypeStruct((slots, rows.shape[1]), F32),
            jax.ShapeDtypeStruct((LANES, LANES), F32),
        ],
        compiler_params=params(32),
        name="route",
    )(ids, table, labels, rows)


def margin_chunk(weight, feat_ref, start, size):
    columns = feat_ref.shape[1]
    half = columns // 2
    matrix = dot(weight[:, :half].astype(BF16), feat_ref[start : start + size, :half], NT)
    sums = []
    sub = 64
    for first in range(start, start + size, sub):
        total = None
        for column in range(half, columns, LANES):
            term = feat_ref[first : first + sub, column : column + LANES].astype(F32) * weight[
                0:1, column : column + LANES
            ]
            total = term if total is None else total + term
        sums.append(total)
    high, low = split(jnp.concatenate(sums, axis=0))
    ones = jnp.ones((8, LANES), BF16)
    return matrix + dot(ones, high, NT) + dot(ones, low, NT)


def margin_kernel(weight_ref, feat_hbm, margin_ref, feat_ref, sems, *, chunks):
    size = feat_ref.shape[0] // chunks
    copies = [
        pltpu.make_async_copy(
            feat_hbm.at[pl.ds(i * size, size)], feat_ref.at[pl.ds(i * size, size)], sems.at[i]
        )
        for i in range(chunks)
    ]
    for copy in copies:
        copy.start()
    weight = jnp.broadcast_to(weight_ref[...].astype(BF16).astype(F32), (8, weight_ref.shape[1]))
    for i in range(chunks):
        copies[i].wait()
        margin_ref[:, i * size : (i + 1) * size] = margin_chunk(weight, feat_ref, i * size, size)[0:1]


def margin_pass(weight, features):
    rows, columns = features.shape
    chunks = 8
    return pl.pallas_call(
        functools.partial(margin_kernel, chunks=chunks),
        in_specs=[VMEM_SPEC, pl.BlockSpec(memory_space=pl.ANY)],
        out_specs=[VMEM_SPEC, VMEM_SPEC],
        out_shape=[jax.ShapeDtypeStruct((1, rows), F32), pltpu.VMEM((rows, columns), BF16)],
        scratch_shapes=[pltpu.SemaphoreType.DMA((chunks,))],
        compiler_params=params(24),
        name="margin",
    )(weight, features)


def grad_kernel(m0, m1, m2, m3, offset_ref, labels_ref, feat_ref, grad_ref):
    margin = (m0[...] + m2[...]) + (m1[...] + m3[...]) + offset_ref[...]
    residual = (jax.nn.sigmoid(margin) - labels_ref[...].astype(F32)).astype(BF16)
    grad_ref[...] = dot(jnp.broadcast_to(residual, (8, residual.shape[1])), feat_ref[...], NN)[0:1]


def grad_pass(margins, offset, labels, features):
    columns = features.shape[1]
    return pl.pallas_call(
        grad_kernel,
        in_specs=[VMEM_SPEC] * 7,
        out_specs=VMEM_SPEC,
        out_shape=jax.ShapeDtypeStruct((1, columns), F32),
        compiler_params=params(24),
        name="grad",
    )(*margins, offset, labels, pltpu.with_memory_space_constraint(features, pltpu.VMEM))


def new_kernel(
    me_ref, g0, g1, g2, g3, weight_ref, meta_ref, t0, t1, t2, t3, feat_ref, updated_ref, send_ref, *, examples
):
    gradient = ((g0[...] + g2[...]) + (g1[...] + g3[...])) / examples + RIDGE_FIXED * weight_ref[...]
    updated = weight_ref[...] - STEP_FIXED * gradient
    updated_ref[...] = updated
    weight = jnp.broadcast_to(updated.astype(BF16).astype(F32), (8, updated.shape[1]))
    mine = me_ref[0]
    block = t0.shape[1]
    send = meta_ref[...]
    for hop, target_ref in enumerate((t0, t1, t2, t3)):
        number = lax.rem(mine - hop + 4, 4)
        pieces = []
        size = 256
        first = pl.multiple_of(number * block, block)
        for start in range(0, block, size):
            pieces.append(margin_chunk(weight, feat_ref.at[pl.ds(first + start, size)], 0, size)[0:1])
        scores = jnp.concatenate(pieces, axis=1)
        target = target_ref[...]
        owner = target // CAPACITY
        lane = number * CAPACITY + target % CAPACITY
        owner_hot = sublane_iota((LANES, block)) == owner
        spread = jnp.where(owner_hot, scores, 0.0)
        high, low = split(spread)
        lane_hot = hot_rows(LANES, lane)
        both = dot(jnp.concatenate([high, low], axis=0), lane_hot, NT)
        send = send + both[:LANES] + both[LANES:]
    send_ref[...] = send


def new_pass(me, grads, weight, meta, targets, features, examples):
    columns = features.shape[1]
    return pl.pallas_call(
        functools.partial(new_kernel, examples=examples),
        in_specs=[pl.BlockSpec(memory_space=pltpu.SMEM)] + [VMEM_SPEC] * 11,
        out_specs=[VMEM_SPEC] * 2,
        out_shape=[
            jax.ShapeDtypeStruct((1, columns), F32),
            jax.ShapeDtypeStruct((LANES, LANES), F32),
        ],
        compiler_params=params(24),
        name="new",
    )(me, *grads, weight, meta, *targets, pltpu.with_memory_space_constraint(features, pltpu.VMEM))


def prepare_kernel(rows_ref, params_ref, high_ref, low_ref, score_ref):
    high, low = split(rows_ref[...])
    high_ref[...] = high
    low_ref[...] = low
    score_ref[...] = dot_split(params_ref[...], high, low, NT)


def prepare(rows, member_params):
    slots, width = rows.shape
    members = member_params.shape[0]
    return pl.pallas_call(
        prepare_kernel,
        in_specs=[VMEM_SPEC] * 2,
        out_specs=[VMEM_SPEC] * 3,
        out_shape=[
            jax.ShapeDtypeStruct((slots, width), BF16),
            jax.ShapeDtypeStruct((slots, width), BF16),
            jax.ShapeDtypeStruct((members, slots), F32),
        ],
        compiler_params=params(24),
        name="prepare",
    )(rows, member_params)


def to_row(table):
    return jnp.concatenate([table[i : i + 1, :] for i in range(table.shape[0])], axis=1)


def members_kernel(recv_ref, high_ref, low_ref, score_ref, params_ref, counts_ref, out_ref, back_ref):
    tiles = high_ref.shape[0] // LANES
    lane = lane_iota((tiles, LANES))
    even = jnp.zeros((tiles, LANES), F32)
    odd = jnp.zeros((tiles, LANES), F32)
    slots = jnp.zeros((tiles, LANES), F32)
    labels = jnp.zeros((tiles, LANES), F32)
    for q in range(8):
        piece = recv_ref[pl.ds(q, tiles, stride=8), :]
        if q < 4:
            even += piece
        else:
            odd += piece
        here = lane // CAPACITY == q
        slots = jnp.where(here, pltpu.roll(piece, (q * CAPACITY - 4 * CAPACITY) % LANES, 1), slots)
        labels = jnp.where(here, pltpu.roll(piece, (q * CAPACITY - 5 * CAPACITY) % LANES, 1), labels)
    offset = to_row(jnp.where(lane < LANES // 2, even, pltpu.roll(odd, LANES // 2, 1)))
    slot = to_row(slots).astype(jnp.int32)
    label = to_row(labels)
    members = params_ref.shape[0]
    mask = sublane_iota((members, slot.shape[1])) == slot

    def own(value):
        return jnp.sum(jnp.where(mask, value, 0.0), axis=0, keepdims=True)

    high, low = high_ref[...], low_ref[...]
    old = params_ref[...]
    scaling = 1.0 / (counts_ref[...].astype(F32) + 1.0)
    margin = offset + own(score_ref[...])
    probability = jax.nn.sigmoid(margin)
    weight = probability * (1.0 - probability)
    errors = jnp.where(mask, label - probability, 0.0)
    remains = scaling * dot_split(errors, high, low, NN) - RIDGE_MEMBER * old
    direction = remains
    delta = jnp.zeros_like(remains)
    norm_now = jnp.sum(remains * remains, axis=1, keepdims=True)
    for step in range(CG_STEPS):
        along = jnp.where(mask, dot_split(direction, high, low, NT), 0.0)
        weighted = along * weight
        curve = scaling * jnp.sum(weighted * along, axis=1, keepdims=True) + RIDGE_MEMBER * jnp.sum(
            direction * direction, axis=1, keepdims=True
        )
        step_size = norm_now / (curve + TINY)
        delta = delta + step_size * direction
        margin = margin + jnp.sum(along * step_size, axis=0, keepdims=True)
        if step < CG_STEPS - 1:
            image = scaling * dot_split(weighted, high, low, NN) + RIDGE_MEMBER * direction
            remains = remains - step_size * image
            norm_next = jnp.sum(remains * remains, axis=1, keepdims=True)
            direction = remains + (norm_next / (norm_now + TINY)) * direction
            norm_now = norm_next
    out_ref[...] = old + delta
    for t in range(tiles):
        back_ref[8 * t : 8 * t + 8, :] = jnp.broadcast_to(
            margin[:, t * LANES : (t + 1) * LANES], (8, LANES)
        )


def members_pass(recv, high, low, score, member_params, counts):
    return pl.pallas_call(
        members_kernel,
        in_specs=[VMEM_SPEC] * 6,
        out_specs=[VMEM_SPEC] * 2,
        out_shape=[
            jax.ShapeDtypeStruct(member_params.shape, F32),
            jax.ShapeDtypeStruct((LANES, LANES), F32),
        ],
        compiler_params=params(32),
        name="members",
    )(recv, high, low, score, member_params, counts)


def collect_kernel(me_ref, back_ref, target_ref, out_ref):
    target = target_ref[...]
    high, low = split(back_ref[...])
    hot = hot_rows(LANES, target // CAPACITY)
    found = dot(high, hot, TN) + dot(low, hot, TN)
    lane = lax.rem(me_ref[0], 8) * CAPACITY + target % CAPACITY
    here = sublane_iota(found.shape) == lane
    out_ref[...] = jnp.sum(jnp.where(here, found, 0.0), axis=0, keepdims=True)


def collect(me, back, target):
    return pl.pallas_call(
        collect_kernel,
        in_specs=[pl.BlockSpec(memory_space=pltpu.SMEM)] + [VMEM_SPEC] * 2,
        out_specs=VMEM_SPEC,
        out_shape=jax.ShapeDtypeStruct(target.shape, F32),
        compiler_params=params(16),
        name="collect",
    )(me, back, target)


def behind(value, axis):
    size = lax.axis_size(axis)
    return [value] + [
        lax.ppermute(value, axis, [(i, (i + hop) % size) for i in range(size)])
        for hop in range(1, size)
    ]


def other_core(value):
    return lax.ppermute(value, "core", [(0, 1), (1, 0)])


def exchange(table):
    sent = table.reshape(LANES, 1, LANES)
    return lax.all_to_all(sent, ALL, split_axis=0, concat_axis=0, tiled=True).reshape(LANES, LANES)


def body(
    features,
    fixed_weight,
    prior_offset,
    labels,
    impression_member,
    member_position,
    member_counts,
    member_features,
    member_params,
):
    owners = lax.axis_size(ALL)
    mem_dev, width = member_params.shape
    rows = member_features.shape[0]
    examples = features.shape[0] * owners // lax.axis_size("feat")
    place = lax.axis_index("feat")
    me = lax.axis_index(ALL).astype(jnp.int32).reshape(1)
    feat_me = place.astype(jnp.int32).reshape(1)
    weight = fixed_weight[None]
    label_row = labels[None]
    my_labels = lax.dynamic_slice_in_dim(label_row, place * rows, rows, axis=1)

    target, row_buf, meta = route(
        impression_member[None], member_position.reshape(-1, LANES), my_labels, member_features, mem_dev
    )
    got = lax.all_to_all(
        row_buf.reshape(owners, CAPACITY, width), ALL, split_axis=0, concat_axis=0, tiled=True
    ).reshape(owners * CAPACITY, width)
    targets = behind(target, "feat")

    margin, held = margin_pass(weight, features)
    margins = behind(margin, "feat")
    grad = grad_pass(margins, prior_offset[None], label_row, held)
    grad = grad + other_core(grad)
    a, b, c, d = behind(grad, "y")
    grads = behind((a + c) + (b + d), "z")
    updated, send = new_pass(feat_me, grads, weight, meta, targets, held, examples)

    recv = exchange(send)
    high, low, score = prepare(got, member_params)
    updated_params, back = members_pass(recv, high, low, score, member_params, member_counts[:, None])
    total = collect(me, exchange(back), target)
    return updated[0], updated_params, total[0]


def solution(mesh):
    split_mesh = Mesh(mesh.devices.reshape(4, 4, 2, 4), ALL)
    dp = ("z", "y", "core")
    placed = (
        P(dp, "feat"),
        P("feat"),
        P(dp),
        P(dp),
        P(ALL),
        P(),
        P(ALL),
        P(ALL, None),
        P(ALL, None),
    )
    return jax.shard_map(
        body,
        mesh=split_mesh,
        in_specs=placed,
        out_specs=(P("feat"), P(ALL, None), P(ALL)),
        check_vma=False,
    )
```

```python
import functools

import jax
import jax.numpy as jnp
from jax import lax
from jax.experimental import pallas as pl
from jax.experimental.pallas import tpu as pltpu
from jax.sharding import Mesh
from jax.sharding import PartitionSpec as P

RIDGE_FIXED = 0.1
STEP_FIXED = 2.0
RIDGE_MEMBER = 0.25
TINY = 1e-30
CG_STEPS = 3
F32 = jnp.float32
BF16 = jnp.bfloat16
LANES = 128
CAPACITY = 16
LEFT, RIGHT, SIDE, MESSAGE = 0, CAPACITY, 2 * CAPACITY, 2 * CAPACITY + 1
ALL = ("z", "y", "core", "feat")
NN = (((1,), (0,)), ((), ()))
NT = (((1,), (1,)), ((), ()))
TN = (((0,), (0,)), ((), ()))
VMEM_SPEC = pl.BlockSpec(memory_space=pltpu.VMEM)


def dot(left, right, dims):
    return lax.dot_general(left, right, dims, preferred_element_type=F32)


def split(value):
    high = value.astype(BF16)
    return high, (value - high.astype(F32)).astype(BF16)


def dot_split(left, high, low, dims):
    left_high, left_low = split(left)
    rows = left.shape[0]
    both = dot(jnp.concatenate([left_high, left_low], axis=0), high, dims)
    return both[:rows] + both[rows:] + dot(left_high, low, dims)


def sublane_iota(shape):
    return lax.broadcasted_iota(jnp.int32, shape, 0)


def lane_iota(shape):
    return lax.broadcasted_iota(jnp.int32, shape, 1)


def hot_rows(count, index):
    shape = (count, index.shape[1])
    return jnp.where(sublane_iota(shape) == index, 1.0, 0.0).astype(BF16)


def per_owner(row):
    return pl.ds(row, LANES, stride=MESSAGE)


def vmem(vmem_mib):
    return pltpu.CompilerParams(vmem_limit_bytes=vmem_mib << 20)


def margin_chunk(weight, feat_ref, start, size):
    columns = feat_ref.shape[1]
    cut = columns // 2
    matrix = dot(weight[:, :cut].astype(BF16), feat_ref[start : start + size, :cut], NT)[0:1]
    sums = []
    for first in range(start, start + size, LANES):
        parts = []
        for sub in range(first, first + LANES, 64):
            total = None
            for column in range(cut, columns, LANES):
                term = feat_ref[sub : sub + 64, column : column + LANES].astype(F32) * weight[
                    0:1, column : column + LANES
                ]
                total = term if total is None else total + term
            parts.append(total)
        sums.append(jnp.sum(jnp.concatenate(parts, axis=0).T, axis=0, keepdims=True))
    return matrix + jnp.concatenate(sums, axis=1)


def front_kernel(
    ids_hbm,
    table_hbm,
    weight_hbm,
    feat_hbm,
    packet_ref,
    feat_ref,
    route_ref,
    ids_ref,
    table_ref,
    weight_ref,
    small_sems,
    feat_sems,
    *,
    mem_dev,
    chunks,
):
    rows = ids_ref.shape[1]
    small = [
        pltpu.make_async_copy(source, target, small_sems.at[i])
        for i, (source, target) in enumerate(
            ((ids_hbm, ids_ref), (table_hbm, table_ref), (weight_hbm, weight_ref))
        )
    ]
    copies = []
    start = 0
    for i, size in enumerate(chunks):
        here = pl.ds(start, size)
        copies.append(pltpu.make_async_copy(feat_hbm.at[here], feat_ref.at[here], feat_sems.at[i]))
        start += size
    for copy in small + copies:
        copy.start()
    for copy in small:
        copy.wait()

    ids = ids_ref[...]
    table = table_ref[...]
    owner_table = (table // mem_dev).astype(F32).astype(BF16)
    slot_table = (table % mem_dev).astype(F32).astype(BF16)
    both = jnp.concatenate([owner_table, slot_table], axis=1)
    found = dot(both, hot_rows(table.shape[0], ids // LANES), TN)
    low_hot = sublane_iota((LANES, rows)) == ids % LANES
    owner = jnp.sum(jnp.where(low_hot, found[:LANES], 0.0), axis=0, keepdims=True)
    slot = jnp.sum(jnp.where(low_hot, found[LANES:], 0.0), axis=0, keepdims=True)
    owner_hot = sublane_iota((LANES, rows)) == owner.astype(jnp.int32)
    hot = jnp.where(owner_hot, 1.0, 0.0).astype(BF16)
    earlier = jnp.where(sublane_iota((rows, rows)) < lane_iota((rows, rows)), 1.0, 0.0).astype(BF16)
    before = dot(hot, earlier, NN)
    rank = jnp.sum(jnp.where(owner_hot, before, 0.0), axis=0, keepdims=True)
    route_ref[0:1, :] = owner
    route_ref[1:2, :] = rank
    route_ref[2:3, :] = slot

    packet_ref[:, feat_ref.shape[0] :] = owner * CAPACITY + rank
    weight = jnp.broadcast_to(weight_ref[...].astype(BF16).astype(F32), (8, weight_ref.shape[1]))
    start = 0
    for copy, size in zip(copies, chunks):
        copy.wait()
        packet_ref[:, start : start + size] = margin_chunk(weight, feat_ref, start, size)
        start += size


def front(ids, table, weight, features, mem_dev):
    rows = ids.shape[1]
    examples, columns = features.shape
    chunks = (examples // 2, examples // 4, examples // 4)
    arguments = (ids, table, weight, features)
    return pl.pallas_call(
        functools.partial(front_kernel, mem_dev=mem_dev, chunks=chunks),
        in_specs=[pl.BlockSpec(memory_space=pl.ANY)] * 4,
        out_specs=[VMEM_SPEC] * 3,
        out_shape=[
            jax.ShapeDtypeStruct((1, examples + rows), F32),
            pltpu.VMEM((examples, columns), BF16),
            pltpu.VMEM((8, rows), F32),
        ],
        scratch_shapes=[
            pltpu.VMEM(ids.shape, jnp.int32),
            pltpu.VMEM(table.shape, jnp.int32),
            pltpu.VMEM(weight.shape, F32),
            pltpu.SemaphoreType.DMA((3,)),
            pltpu.SemaphoreType.DMA((len(chunks),)),
        ],
        compiler_params=vmem(16),
        name="front",
    )(*(pltpu.with_memory_space_constraint(argument, pltpu.HBM) for argument in arguments))


def place_kernel(route_ref, labels_ref, rows_ref, buf_hbm, meta_ref, buf_ref, sem):
    rows, width = rows_ref.shape
    owner = route_ref[0:1, :].astype(jnp.int32)
    rank = route_ref[1:2, :].astype(jnp.int32)
    slot = route_ref[2:3, :]
    first = pl.multiple_of(lax.axis_index("feat") * rows, rows)
    labels = labels_ref[:, pl.ds(first, rows)].astype(F32)
    owner_hot = sublane_iota((LANES, rows)) == owner
    high, low = split(rows_ref[...])
    parts = jnp.concatenate([high, low], axis=1)
    group = 8
    for base in range(0, CAPACITY, group):
        place = [jnp.where(owner_hot & (rank == base + i), 1.0, 0.0).astype(BF16) for i in range(group)]
        moved = dot(jnp.concatenate(place, axis=0), parts, NN)
        moved = moved[:, :width] + moved[:, width:]
        for i in range(group):
            here = slice(i * LANES, (i + 1) * LANES)
            buf_ref[per_owner(LEFT + base + i), :] = moved[here, :LANES]
            buf_ref[per_owner(RIGHT + base + i), :] = moved[here, LANES:]
    buf_ref[per_owner(SIDE), :] = jnp.zeros((LANES, LANES), F32)
    out = pltpu.make_async_copy(buf_ref, buf_hbm, sem)
    out.start()
    slot_hot = jnp.where(owner_hot, slot, 0.0).astype(BF16)
    label_hot = jnp.where(owner_hot, labels, 0.0).astype(BF16)
    meta_ref[...] = dot(slot_hot, hot_rows(LANES, rank + 4 * CAPACITY), NT) + dot(
        label_hot, hot_rows(LANES, rank + 5 * CAPACITY), NT
    )
    out.wait()


def place(routes, labels, member_rows):
    buf = (LANES * MESSAGE, LANES)
    return pl.pallas_call(
        place_kernel,
        in_specs=[VMEM_SPEC] * 3,
        out_specs=[pl.BlockSpec(memory_space=pltpu.HBM), VMEM_SPEC],
        out_shape=[pltpu.HBM(buf, F32), jax.ShapeDtypeStruct((LANES, LANES), F32)],
        scratch_shapes=[pltpu.VMEM(buf, F32), pltpu.SemaphoreType.DMA],
        compiler_params=vmem(16),
        name="place",
    )(routes, labels, member_rows)


def grad_kernel(
    p0, p1, p2, p3, offset_ref, labels_ref, feat_ref, meta_ref, grad_hbm, owner_ref, lane_ref, copies_ref, sem
):
    count = offset_ref.shape[1]
    margin = (p0[:, :count] + p2[:, :count]) + (p1[:, :count] + p3[:, :count]) + offset_ref[...]
    residual = (jax.nn.sigmoid(margin) - labels_ref[...].astype(F32)).astype(BF16)
    grad = dot(jnp.broadcast_to(residual, (8, count)), feat_ref[...], NN)[0:1]
    copies_ref[...] = jnp.broadcast_to(grad[None], copies_ref.shape)
    out = pltpu.make_async_copy(copies_ref, grad_hbm, sem)
    out.start()
    block = p0.shape[1] - count
    for hop, packet_ref in enumerate((p0, p1, p2, p3)):
        number = lax.rem(lax.axis_index("feat") - hop + 4, 4)
        target = packet_ref[:, count:].astype(jnp.int32)
        here = pl.ds(pl.multiple_of(number * block, block), block)
        owner_ref[:, here] = hot_rows(LANES, target // CAPACITY)
        lane_ref[:, here] = hot_rows(LANES, number * CAPACITY + target % CAPACITY)
    out.wait()


def grad_pass(packets, offset, labels, features, meta, peers):
    examples, columns = features.shape
    shape = (peers, 1, columns)
    return pl.pallas_call(
        grad_kernel,
        in_specs=[VMEM_SPEC] * 7 + [pl.BlockSpec(memory_space=pl.ANY)],
        out_specs=[pl.BlockSpec(memory_space=pltpu.HBM), VMEM_SPEC, VMEM_SPEC],
        out_shape=[pltpu.HBM(shape, F32)] + [jax.ShapeDtypeStruct((LANES, examples), BF16)] * 2,
        scratch_shapes=[pltpu.VMEM(shape, F32), pltpu.SemaphoreType.DMA],
        compiler_params=vmem(16),
        name="grad",
    )(*packets, offset, labels, pltpu.with_memory_space_constraint(features, pltpu.VMEM), meta)


def new_kernel(
    grads_ref,
    weight_ref,
    meta_ref,
    owner_ref,
    lane_ref,
    feat_ref,
    buf_hbm,
    updated_ref,
    send_hbm,
    buf_ref,
    sems,
    *,
    examples,
):
    into = pltpu.make_async_copy(buf_hbm, buf_ref, sems.at[0])
    into.start()
    gradient = jnp.sum(grads_ref[...], axis=0) / examples + RIDGE_FIXED * weight_ref[...]
    updated = weight_ref[...] - STEP_FIXED * gradient
    updated_ref[...] = updated
    weight = jnp.broadcast_to(updated.astype(BF16).astype(F32), (8, updated.shape[1]))
    count = feat_ref.shape[0]
    size = 512
    send = meta_ref[...]
    for start in range(0, count, size):
        here = slice(start, start + size)
        high, low = split(margin_chunk(weight, feat_ref, start, size))
        owner_hot = owner_ref[:, here]
        both = dot(jnp.concatenate([owner_hot * high, owner_hot * low], axis=0), lane_ref[:, here], NT)
        send = send + both[:LANES] + both[LANES:]
    into.wait()
    buf_ref[per_owner(SIDE), :] = send
    out = pltpu.make_async_copy(buf_ref, send_hbm, sems.at[1])
    out.start()
    out.wait()


def new_pass(grads, weight, meta, owner_hot, lane_hot, features, row_buf, examples):
    columns = features.shape[1]
    return pl.pallas_call(
        functools.partial(new_kernel, examples=examples),
        in_specs=[VMEM_SPEC] * 6 + [pl.BlockSpec(memory_space=pl.ANY)],
        out_specs=[VMEM_SPEC, pl.BlockSpec(memory_space=pltpu.HBM)],
        out_shape=[jax.ShapeDtypeStruct((1, columns), F32), pltpu.HBM(row_buf.shape, F32)],
        scratch_shapes=[pltpu.VMEM(row_buf.shape, F32), pltpu.SemaphoreType.DMA((2,))],
        compiler_params=vmem(16),
        name="new",
    )(
        grads,
        weight,
        meta,
        owner_hot,
        lane_hot,
        pltpu.with_memory_space_constraint(features, pltpu.VMEM),
        pltpu.with_memory_space_constraint(row_buf, pltpu.HBM),
    )


def to_row(table):
    return jnp.concatenate([table[i : i + 1, :] for i in range(table.shape[0])], axis=1)


def members_kernel(recv_ref, params_ref, counts_ref, out_ref, back_ref, high_ref, low_ref):
    for k in range(CAPACITY):
        rows = jnp.concatenate([recv_ref[per_owner(LEFT + k), :], recv_ref[per_owner(RIGHT + k), :]], axis=1)
        here = pl.ds(k * LANES, LANES)
        high_ref[here, :], low_ref[here, :] = split(rows)
    side = recv_ref[per_owner(SIDE), :].T
    groups = lax.axis_size("feat")
    lane = lane_iota((CAPACITY, LANES))
    offsets = jnp.zeros((CAPACITY, LANES), F32)
    for block in range(groups):
        part = side[block * CAPACITY : (block + 1) * CAPACITY]
        whole = part
        for hop in range(1, groups):
            whole = whole + pltpu.roll(part, hop, 1)
        whole = pltpu.roll(whole, (block - groups + 1) % LANES, 1)
        offsets = jnp.where(lane % groups == block, whole, offsets)
    offset = to_row(offsets)
    slot = to_row(side[4 * CAPACITY : 5 * CAPACITY]).astype(jnp.int32)
    label = to_row(side[5 * CAPACITY : 6 * CAPACITY])
    members = params_ref.shape[0]
    mask = sublane_iota((members, slot.shape[1])) == slot

    def own(value):
        return jnp.sum(jnp.where(mask, value, 0.0), axis=0, keepdims=True)

    high, low = high_ref[...], low_ref[...]
    old = params_ref[...]
    scaling = 1.0 / (counts_ref[...].astype(F32) + 1.0)
    margin = offset + own(dot_split(old, high, low, NT))
    probability = jax.nn.sigmoid(margin)
    weight = probability * (1.0 - probability)
    errors = jnp.where(mask, label - probability, 0.0)
    remains = scaling * dot_split(errors, high, low, NN) - RIDGE_MEMBER * old
    direction = remains
    delta = jnp.zeros_like(remains)
    norm_now = jnp.sum(remains * remains, axis=1, keepdims=True)
    for step in range(CG_STEPS):
        along = jnp.where(mask, dot_split(direction, high, low, NT), 0.0)
        weighted = along * weight
        curve = scaling * jnp.sum(weighted * along, axis=1, keepdims=True) + RIDGE_MEMBER * jnp.sum(
            direction * direction, axis=1, keepdims=True
        )
        step_size = norm_now / (curve + TINY)
        delta = delta + step_size * direction
        margin = margin + jnp.sum(along * step_size, axis=0, keepdims=True)
        if step < CG_STEPS - 1:
            image = scaling * dot_split(weighted, high, low, NN) + RIDGE_MEMBER * direction
            remains = remains - step_size * image
            norm_next = jnp.sum(remains * remains, axis=1, keepdims=True)
            direction = remains + (norm_next / (norm_now + TINY)) * direction
            norm_now = norm_next
    out_ref[...] = old + delta
    table = jnp.concatenate(
        [margin[:, k * LANES : (k + 1) * LANES] for k in range(CAPACITY)]
        + [jnp.zeros((LANES - CAPACITY, LANES), F32)],
        axis=0,
    )
    back_ref[...] = table.T


def members_pass(recv, member_params, counts):
    members, width = member_params.shape
    held = pltpu.VMEM((LANES * CAPACITY, width), BF16)
    return pl.pallas_call(
        members_kernel,
        in_specs=[VMEM_SPEC] * 3,
        out_specs=[VMEM_SPEC] * 2,
        out_shape=[
            jax.ShapeDtypeStruct(member_params.shape, F32),
            jax.ShapeDtypeStruct((LANES, LANES), F32),
        ],
        scratch_shapes=[held, held],
        compiler_params=vmem(16),
        name="members",
    )(recv, member_params, counts)


def collect_kernel(back_ref, route_ref, out_ref):
    high, low = split(back_ref[...])
    hot = hot_rows(LANES, route_ref[0:1, :].astype(jnp.int32))
    found = dot(high, hot, TN) + dot(low, hot, TN)
    here = sublane_iota(found.shape) == route_ref[1:2, :].astype(jnp.int32)
    out_ref[...] = jnp.sum(jnp.where(here, found, 0.0), axis=0, keepdims=True)


def collect(back, routes):
    return pl.pallas_call(
        collect_kernel,
        in_specs=[VMEM_SPEC] * 2,
        out_specs=VMEM_SPEC,
        out_shape=jax.ShapeDtypeStruct((1, routes.shape[1]), F32),
        compiler_params=vmem(8),
        name="collect",
    )(back, routes)


def behind(value, axis):
    size = lax.axis_size(axis)
    return [value] + [
        lax.ppermute(value, axis, [(i, (i + hop) % size) for i in range(size)])
        for hop in range(1, size)
    ]


def gather(copies, axes):
    return lax.all_to_all(copies, axes, split_axis=0, concat_axis=0, tiled=True)


def exchange(table):
    sent = table.reshape(LANES, 1, -1)
    got = lax.all_to_all(sent, ALL, split_axis=0, concat_axis=0, tiled=True)
    return got.reshape(table.shape)


def body(
    features,
    fixed_weight,
    prior_offset,
    labels,
    impression_member,
    member_position,
    member_counts,
    member_features,
    member_params,
):
    owners = lax.axis_size(ALL)
    mem_dev = member_params.shape[0]
    examples = features.shape[0] * owners // lax.axis_size("feat")
    weight = fixed_weight[None]
    label_row = labels[None]

    packet, held, routes = front(
        impression_member[None],
        member_position.reshape(-1, LANES),
        weight,
        features,
        mem_dev,
    )
    packets = behind(packet, "feat")
    row_buf, meta = place(routes, label_row, member_features)
    dp = ("z", "y", "core")
    grad, owner_hot, lane_hot = grad_pass(
        packets, prior_offset[None], label_row, held, meta, lax.axis_size(dp)
    )
    grads = gather(grad, dp)
    updated, send = new_pass(grads, weight, meta, owner_hot, lane_hot, held, row_buf, examples)
    updated_params, back = members_pass(exchange(send), member_params, member_counts[:, None])
    total = collect(exchange(back), routes)
    return updated[0], updated_params, total[0]


def solution(mesh):
    split_mesh = Mesh(mesh.devices.reshape(4, 4, 2, 4), ALL)
    dp = ("z", "y", "core")
    placed = (
        P(dp, "feat"),
        P("feat"),
        P(dp),
        P(dp),
        P(ALL),
        P(),
        P(ALL),
        P(ALL, None),
        P(ALL, None),
    )
    return jax.shard_map(
        body,
        mesh=split_mesh,
        in_specs=placed,
        out_specs=(P("feat"), P(ALL, None), P(ALL)),
        check_vma=False,
    )
```

```python
import functools

import jax
import jax.numpy as jnp
from jax import lax
from jax.experimental import pallas as pl
from jax.experimental.pallas import tpu as pltpu
from jax.sharding import Mesh
from jax.sharding import PartitionSpec as P

RIDGE_FIXED = 0.1
STEP_FIXED = 2.0
RIDGE_MEMBER = 0.25
TINY = 1e-30
CG_STEPS = 3
F32 = jnp.float32
BF16 = jnp.bfloat16
LANES = 128
CAPACITY = 16
LEFT, RIGHT, SIDE, MESSAGE = 0, CAPACITY, 2 * CAPACITY, 2 * CAPACITY + 1
ALL = ("z", "y", "core", "feat")
NN = (((1,), (0,)), ((), ()))
NT = (((1,), (1,)), ((), ()))
TN = (((0,), (0,)), ((), ()))
VMEM_SPEC = pl.BlockSpec(memory_space=pltpu.VMEM)


def dot(left, right, dims):
    return lax.dot_general(left, right, dims, preferred_element_type=F32)


def split(value):
    high = value.astype(BF16)
    return high, (value - high.astype(F32)).astype(BF16)


def dot_split(left, high, low, dims):
    left_high, left_low = split(left)
    rows = left.shape[0]
    both = dot(jnp.concatenate([left_high, left_low], axis=0), high, dims)
    total = both[:rows] + both[rows:]
    return total if low is None else total + dot(left_high, low, dims)


def sublane_iota(shape):
    return lax.broadcasted_iota(jnp.int32, shape, 0)


def lane_iota(shape):
    return lax.broadcasted_iota(jnp.int32, shape, 1)


def hot_rows(count, index):
    number = sublane_iota((count, LANES)).astype(F32).astype(BF16)
    index = index.astype(F32).astype(BF16)
    one, zero = jnp.ones((), BF16), jnp.zeros((), BF16)
    return jnp.concatenate(
        [
            jnp.where(number == index[:, start : start + LANES], one, zero)
            for start in range(0, index.shape[1], LANES)
        ],
        axis=1,
    )


def per_owner(row):
    return pl.ds(row, LANES, stride=MESSAGE)


def vmem(vmem_mib):
    return pltpu.CompilerParams(vmem_limit_bytes=vmem_mib << 20)


def margin_chunk(weight, feat_ref, start, size):
    columns = feat_ref.shape[1]
    cut = columns // 2
    matrix = dot(weight[:, :cut].astype(BF16), feat_ref[start : start + size, :cut], NT)[0:1]
    sums = []
    for first in range(start, start + size, LANES):
        parts = []
        for sub in range(first, first + LANES, 64):
            total = None
            for column in range(cut, columns, LANES):
                term = feat_ref[sub : sub + 64, column : column + LANES].astype(F32) * weight[
                    0:1, column : column + LANES
                ]
                total = term if total is None else total + term
            parts.append(total)
        sums.append(jnp.sum(jnp.concatenate(parts, axis=0).T, axis=0, keepdims=True))
    return matrix + jnp.concatenate(sums, axis=1)


def front_kernel(
    ids_hbm,
    table_hbm,
    weight_hbm,
    feat_hbm,
    packet_ref,
    feat_ref,
    route_ref,
    ids_ref,
    table_ref,
    weight_ref,
    small_sems,
    feat_sems,
    *,
    mem_dev,
    chunks,
):
    rows = ids_ref.shape[1]
    small = [
        pltpu.make_async_copy(source, target, small_sems.at[i])
        for i, (source, target) in enumerate(
            ((ids_hbm, ids_ref), (table_hbm, table_ref), (weight_hbm, weight_ref))
        )
    ]
    copies = []
    start = 0
    for i, size in enumerate(chunks):
        here = pl.ds(start, size)
        copies.append(pltpu.make_async_copy(feat_hbm.at[here], feat_ref.at[here], feat_sems.at[i]))
        start += size
    for copy in small + copies:
        copy.start()
    for copy in small:
        copy.wait()

    ids = ids_ref[...]
    table = table_ref[...]
    owner_table = (table // mem_dev).astype(F32).astype(BF16)
    slot_table = (table % mem_dev).astype(F32).astype(BF16)
    both = jnp.concatenate([owner_table, slot_table], axis=1)
    found = dot(both, hot_rows(table.shape[0], ids // LANES), TN)
    low_hot = sublane_iota((LANES, rows)) == ids % LANES
    owner = jnp.sum(jnp.where(low_hot, found[:LANES], 0.0), axis=0, keepdims=True)
    slot = jnp.sum(jnp.where(low_hot, found[LANES:], 0.0), axis=0, keepdims=True)
    owner_hot = sublane_iota((LANES, rows)) == owner.astype(jnp.int32)
    hot = jnp.where(owner_hot, 1.0, 0.0).astype(BF16)
    earlier = jnp.where(sublane_iota((rows, rows)) < lane_iota((rows, rows)), 1.0, 0.0).astype(BF16)
    before = dot(hot, earlier, NN)
    rank = jnp.sum(jnp.where(owner_hot, before, 0.0), axis=0, keepdims=True)
    route_ref[0:1, :] = owner
    route_ref[1:2, :] = rank
    route_ref[2:3, :] = slot

    packet_ref[:, feat_ref.shape[0] :] = owner * CAPACITY + rank
    weight = jnp.broadcast_to(weight_ref[...].astype(BF16).astype(F32), (8, weight_ref.shape[1]))
    start = 0
    for copy, size in zip(copies, chunks):
        copy.wait()
        packet_ref[:, start : start + size] = margin_chunk(weight, feat_ref, start, size)
        start += size


def front(ids, table, weight, features, mem_dev):
    rows = ids.shape[1]
    examples, columns = features.shape
    chunks = (examples // 2, examples // 2)
    arguments = (ids, table, weight, features)
    return pl.pallas_call(
        functools.partial(front_kernel, mem_dev=mem_dev, chunks=chunks),
        in_specs=[pl.BlockSpec(memory_space=pl.ANY)] * 4,
        out_specs=[VMEM_SPEC] * 3,
        out_shape=[
            jax.ShapeDtypeStruct((1, examples + rows), F32),
            pltpu.VMEM((examples, columns), BF16),
            pltpu.VMEM((8, rows), F32),
        ],
        scratch_shapes=[
            pltpu.VMEM(ids.shape, jnp.int32),
            pltpu.VMEM(table.shape, jnp.int32),
            pltpu.VMEM(weight.shape, F32),
            pltpu.SemaphoreType.DMA((3,)),
            pltpu.SemaphoreType.DMA((len(chunks),)),
        ],
        compiler_params=vmem(16),
        name="front",
    )(*(pltpu.with_memory_space_constraint(argument, pltpu.HBM) for argument in arguments))


def place_kernel(route_ref, labels_ref, rows_ref, buf_ref, meta_ref):
    rows, width = rows_ref.shape
    owner = route_ref[0:1, :].astype(jnp.int32)
    rank = route_ref[1:2, :].astype(jnp.int32)
    slot = route_ref[2:3, :]
    first = pl.multiple_of(lax.axis_index("feat") * rows, rows)
    labels = labels_ref[:, pl.ds(first, rows)].astype(F32)
    owner_hot = hot_rows(LANES, owner)
    high, low = split(rows_ref[...])
    parts = jnp.concatenate([high, low], axis=1)
    group = 8
    for base in range(0, CAPACITY, group):
        place = [owner_hot * jnp.where(rank == base + i, 1.0, 0.0).astype(BF16) for i in range(group)]
        moved = dot(jnp.concatenate(place, axis=0), parts, NN)
        moved = moved[:, :width] + moved[:, width:]
        for i in range(group):
            here = slice(i * LANES, (i + 1) * LANES)
            buf_ref[per_owner(LEFT + base + i), :] = moved[here, :LANES]
            buf_ref[per_owner(RIGHT + base + i), :] = moved[here, LANES:]
    buf_ref[per_owner(SIDE), :] = jnp.zeros((LANES, LANES), F32)
    slot_hot = owner_hot * slot.astype(BF16)
    label_hot = owner_hot * labels.astype(BF16)
    meta_ref[...] = dot(slot_hot, hot_rows(LANES, rank + 4 * CAPACITY), NT) + dot(
        label_hot, hot_rows(LANES, rank + 5 * CAPACITY), NT
    )


def place(routes, labels, member_rows):
    buf = (LANES * MESSAGE, LANES)
    return pl.pallas_call(
        place_kernel,
        in_specs=[VMEM_SPEC] * 3,
        out_specs=[VMEM_SPEC] * 2,
        out_shape=[pltpu.VMEM(buf, F32), jax.ShapeDtypeStruct((LANES, LANES), F32)],
        compiler_params=vmem(16),
        name="place",
    )(routes, labels, member_rows)


def to_row(table):
    return jnp.concatenate([table[i : i + 1, :] for i in range(table.shape[0])], axis=1)


def to_table(row):
    return jnp.concatenate([row[:, i : i + LANES] for i in range(0, row.shape[1], LANES)], axis=0)


def grad_kernel(
    p0,
    p1,
    p2,
    p3,
    offset_ref,
    labels_ref,
    feat_ref,
    meta_ref,
    copies_ref,
    owner_ref,
    lane_ref,
):
    count = offset_ref.shape[1]
    block = p0.shape[1] - count
    for hop, packet_ref in enumerate((p0, p1, p2, p3)):
        number = lax.rem(lax.axis_index("feat") - hop + 4, 4)
        target = packet_ref[:, count:].astype(jnp.int32)
        here = pl.ds(pl.multiple_of(number * block, block), block)
        owner_ref[:, here] = hot_rows(LANES, target // CAPACITY)
        lane_ref[:, here] = hot_rows(LANES, number * CAPACITY + target % CAPACITY)
    margin = (p0[:, :count] + p2[:, :count]) + (p1[:, :count] + p3[:, :count]) + offset_ref[...]
    residual = (jax.nn.sigmoid(margin) - labels_ref[...].astype(F32)).astype(BF16)
    grad = dot(jnp.broadcast_to(residual, (8, count)), feat_ref[...], NN)[0:1]
    copies_ref[...] = jnp.broadcast_to(to_table(grad)[None], copies_ref.shape)


def grad_pass(packets, offset, labels, features, meta, peers):
    examples, columns = features.shape
    shape = (peers, columns // LANES, LANES)
    return pl.pallas_call(
        grad_kernel,
        in_specs=[VMEM_SPEC] * 7 + [pl.BlockSpec(memory_space=pl.ANY)],
        out_specs=[VMEM_SPEC] * 3,
        out_shape=[pltpu.VMEM(shape, F32)] + [pltpu.VMEM((LANES, examples), BF16)] * 2,
        compiler_params=vmem(16),
        name="grad",
    )(
        *packets,
        offset,
        labels,
        pltpu.with_memory_space_constraint(features, pltpu.VMEM),
        meta,
    )


def new_kernel(
    grads_ref,
    weight_ref,
    meta_ref,
    owner_ref,
    lane_ref,
    feat_ref,
    buf_ref,
    updated_hbm,
    send_ref,
    updated_ref,
    sem,
    *,
    examples,
):
    gradient = to_row(jnp.sum(grads_ref[...], axis=0)) / examples + RIDGE_FIXED * weight_ref[...]
    updated = weight_ref[...] - STEP_FIXED * gradient
    updated_ref[...] = updated
    result = pltpu.make_async_copy(updated_ref, updated_hbm, sem)
    result.start()
    weight = jnp.broadcast_to(updated.astype(BF16).astype(F32), (8, updated.shape[1]))
    count = feat_ref.shape[0]
    size = 512
    send = meta_ref[...]
    for start in range(0, count, size):
        here = slice(start, start + size)
        high, low = split(margin_chunk(weight, feat_ref, start, size))
        owner_hot = owner_ref[:, here]
        both = dot(jnp.concatenate([owner_hot * high, owner_hot * low], axis=0), lane_ref[:, here], NT)
        send = send + both[:LANES] + both[LANES:]
    send_ref[per_owner(SIDE), :] = send
    result.wait()


def new_pass(grads, weight, meta, owner_hot, lane_hot, features, row_buf, examples):
    columns = features.shape[1]
    return pl.pallas_call(
        functools.partial(new_kernel, examples=examples),
        in_specs=[VMEM_SPEC] * 7,
        out_specs=[pl.BlockSpec(memory_space=pltpu.HBM), VMEM_SPEC],
        out_shape=[pltpu.HBM((1, columns), F32), pltpu.VMEM(row_buf.shape, F32)],
        input_output_aliases={6: 1},
        scratch_shapes=[pltpu.VMEM((1, columns), F32), pltpu.SemaphoreType.DMA],
        compiler_params=vmem(16),
        name="new",
    )(
        grads,
        weight,
        meta,
        owner_hot,
        lane_hot,
        pltpu.with_memory_space_constraint(features, pltpu.VMEM),
        pltpu.with_memory_space_constraint(row_buf, pltpu.VMEM),
    )


def members_kernel(
    recv_ref, params_ref, counts_ref, route_hbm, out_ref, back_ref, route_ref, high_ref, low_ref, sem
):
    keep = pltpu.make_async_copy(route_hbm, route_ref, sem)
    keep.start()
    for k in range(CAPACITY):
        rows = jnp.concatenate([recv_ref[per_owner(LEFT + k), :], recv_ref[per_owner(RIGHT + k), :]], axis=1)
        here = pl.ds(k * LANES, LANES)
        high_ref[here, :], low_ref[here, :] = split(rows)
    side = recv_ref[per_owner(SIDE), :].T
    groups = lax.axis_size("feat")
    lane = lane_iota((CAPACITY, LANES))
    offsets = jnp.zeros((CAPACITY, LANES), F32)
    for block in range(groups):
        part = side[block * CAPACITY : (block + 1) * CAPACITY]
        whole = part
        for hop in range(1, groups):
            whole = whole + pltpu.roll(part, hop, 1)
        whole = pltpu.roll(whole, (block - groups + 1) % LANES, 1)
        offsets = jnp.where(lane % groups == block, whole, offsets)
    offset = to_row(offsets)
    slot = to_row(side[4 * CAPACITY : 5 * CAPACITY]).astype(jnp.int32)
    label = to_row(side[5 * CAPACITY : 6 * CAPACITY])
    members = params_ref.shape[0]
    mask = sublane_iota((members, slot.shape[1])) == slot

    def own(value):
        return jnp.sum(jnp.where(mask, value, 0.0), axis=0, keepdims=True)

    high, low = high_ref[...], low_ref[...]
    old = params_ref[...]
    diagonal = sublane_iota((members, members)) == lane_iota((members, members))
    scales = jnp.broadcast_to(1.0 / (counts_ref[...].astype(F32) + 1.0), (members, members))
    scaling = jnp.sum(jnp.where(diagonal, scales, 0.0), axis=1, keepdims=True)
    margin = offset + own(dot_split(old, high, low, NT))
    probability = jax.nn.sigmoid(margin)
    weight = probability * (1.0 - probability)
    errors = jnp.where(mask, label - probability, 0.0)
    remains = scaling * dot_split(errors, high, low, NN) - RIDGE_MEMBER * old
    direction = remains
    delta = jnp.zeros_like(remains)
    norm_now = jnp.sum(remains * remains, axis=1, keepdims=True)
    for step in range(CG_STEPS):
        along = jnp.where(mask, dot_split(direction, high, None if step == 2 else low, NT), 0.0)
        weighted = along * weight
        curve = scaling * jnp.sum(weighted * along, axis=1, keepdims=True) + RIDGE_MEMBER * jnp.sum(
            direction * direction, axis=1, keepdims=True
        )
        step_size = norm_now / (curve + TINY)
        delta = delta + step_size * direction
        margin = margin + jnp.sum(along * step_size, axis=0, keepdims=True)
        if step < CG_STEPS - 1:
            image = scaling * dot_split(weighted, high, None if step == 1 else low, NN) + RIDGE_MEMBER * direction
            remains = remains - step_size * image
            norm_next = jnp.sum(remains * remains, axis=1, keepdims=True)
            direction = remains + (norm_next / (norm_now + TINY)) * direction
            norm_now = norm_next
    out_ref[...] = old + delta
    table = jnp.concatenate(
        [margin[:, k * LANES : (k + 1) * LANES] for k in range(CAPACITY)]
        + [jnp.zeros((LANES - CAPACITY, LANES), F32)],
        axis=0,
    )
    back_ref[...] = table.T
    keep.wait()


def members_pass(recv, member_params, counts, routes):
    members, width = member_params.shape
    held = pltpu.VMEM((LANES * CAPACITY, width), BF16)
    return pl.pallas_call(
        members_kernel,
        in_specs=[VMEM_SPEC] * 3 + [pl.BlockSpec(memory_space=pl.ANY)],
        out_specs=[VMEM_SPEC] * 3,
        out_shape=[
            pltpu.VMEM(member_params.shape, F32),
            jax.ShapeDtypeStruct((LANES, LANES), F32),
            pltpu.VMEM(routes.shape, F32),
        ],
        scratch_shapes=[held, held, pltpu.SemaphoreType.DMA],
        compiler_params=vmem(16),
        name="members",
    )(recv, member_params, counts, routes)


def collect_kernel(back_ref, route_ref, params_ref, out_ref, params_hbm, sem):
    result = pltpu.make_async_copy(params_ref, params_hbm, sem)
    result.start()
    high, low = split(back_ref[:, :CAPACITY])
    hot = hot_rows(LANES, route_ref[0:1, :].astype(jnp.int32))
    found = dot(jnp.concatenate([high, low], axis=0), jnp.concatenate([hot, hot], axis=0), TN)
    here = sublane_iota(found.shape) == route_ref[1:2, :].astype(jnp.int32)
    out_ref[...] = jnp.sum(jnp.where(here, found, 0.0), axis=0, keepdims=True)
    result.wait()


def collect(back, routes, updated_params):
    return pl.pallas_call(
        collect_kernel,
        in_specs=[VMEM_SPEC] * 3,
        out_specs=[VMEM_SPEC, pl.BlockSpec(memory_space=pltpu.HBM)],
        out_shape=[
            jax.ShapeDtypeStruct((1, routes.shape[1]), F32),
            pltpu.HBM(updated_params.shape, F32),
        ],
        scratch_shapes=[pltpu.SemaphoreType.DMA],
        compiler_params=vmem(8),
        name="collect",
    )(back, routes, pltpu.with_memory_space_constraint(updated_params, pltpu.VMEM))


def behind(value, axis):
    size = lax.axis_size(axis)
    return [value] + [
        lax.ppermute(value, axis, [(i, (i + hop) % size) for i in range(size)])
        for hop in range(1, size)
    ]


def gather(copies, axes):
    return lax.all_to_all(copies, axes, split_axis=0, concat_axis=0, tiled=True)


def exchange(table):
    sent = table.reshape(LANES, 1, -1)
    got = lax.all_to_all(sent, ALL, split_axis=0, concat_axis=0, tiled=True)
    return got.reshape(table.shape)


def body(
    features,
    fixed_weight,
    prior_offset,
    labels,
    impression_member,
    member_position,
    member_counts,
    member_features,
    member_params,
):
    owners = lax.axis_size(ALL)
    mem_dev = member_params.shape[0]
    examples = features.shape[0] * owners // lax.axis_size("feat")
    weight = fixed_weight[None]
    label_row = labels[None]

    packet, held, routes = front(
        impression_member[None],
        member_position.reshape(-1, LANES),
        weight,
        features,
        mem_dev,
    )
    packets = behind(packet, "feat")
    row_buf, meta = place(routes, label_row, member_features)
    dp = ("z", "y", "core")
    grad, owner_hot, lane_hot = grad_pass(
        packets, prior_offset[None], label_row, held, meta, lax.axis_size(dp)
    )
    grads = gather(grad, dp)
    updated, send = new_pass(grads, weight, meta, owner_hot, lane_hot, held, row_buf, examples)
    updated_params, back, routes = members_pass(
        exchange(send), member_params, member_counts[None], routes
    )
    total, updated_params = collect(exchange(back), routes, updated_params)
    return updated[0], updated_params, total[0]


def solution(mesh):
    split_mesh = Mesh(mesh.devices.reshape(4, 4, 2, 4), ALL)
    dp = ("z", "y", "core")
    placed = (
        P(dp, "feat"),
        P("feat"),
        P(dp),
        P(dp),
        P(ALL),
        P(),
        P(ALL),
        P(ALL, None),
        P(ALL, None),
    )
    return jax.shard_map(
        body,
        mesh=split_mesh,
        in_specs=placed,
        out_specs=(P("feat"), P(ALL, None), P(ALL)),
        check_vma=False,
    )
```

```python
import functools

import jax
import jax.numpy as jnp
from jax import lax
from jax.experimental import pallas as pl
from jax.experimental.pallas import tpu as pltpu
from jax.sharding import Mesh
from jax.sharding import PartitionSpec as P

RIDGE_FIXED = 0.1
STEP_FIXED = 2.0
RIDGE_MEMBER = 0.25
TINY = 1e-30
CG_STEPS = 3
F32 = jnp.float32
BF16 = jnp.bfloat16
LANES = 128
CAPACITY = 16
LEFT, RIGHT, SIDE, MESSAGE = 0, CAPACITY, 2 * CAPACITY, 2 * CAPACITY + 1
ALL = ("z", "y", "core", "feat")
NN = (((1,), (0,)), ((), ()))
NT = (((1,), (1,)), ((), ()))
TN = (((0,), (0,)), ((), ()))
VMEM_SPEC = pl.BlockSpec(memory_space=pltpu.VMEM)


def dot(left, right, dims):
    return lax.dot_general(left, right, dims, preferred_element_type=F32)


def split(value):
    high = value.astype(BF16)
    return high, (value - high.astype(F32)).astype(BF16)


def dot_split(left, high, low, dims):
    left_high, left_low = split(left)
    rows = left.shape[0]
    both = dot(jnp.concatenate([left_high, left_low], axis=0), high, dims)
    total = both[:rows] + both[rows:]
    return total if low is None else total + dot(left_high, low, dims)


def sublane_iota(shape):
    return lax.broadcasted_iota(jnp.int32, shape, 0)


def lane_iota(shape):
    return lax.broadcasted_iota(jnp.int32, shape, 1)


def hot_rows(count, index):
    number = sublane_iota((count, LANES)).astype(F32).astype(BF16)
    index = index.astype(F32).astype(BF16)
    one, zero = jnp.ones((), BF16), jnp.zeros((), BF16)
    return jnp.concatenate(
        [
            jnp.where(number == index[:, start : start + LANES], one, zero)
            for start in range(0, index.shape[1], LANES)
        ],
        axis=1,
    )


def per_owner(row):
    return pl.ds(row, LANES, stride=MESSAGE)


def vmem(vmem_mib):
    return pltpu.CompilerParams(vmem_limit_bytes=vmem_mib << 20)


def margin_chunk(weight, feat_ref, start, size):
    columns = feat_ref.shape[1]
    cut = columns // 2
    matrix = dot(weight[:, :cut].astype(BF16), feat_ref[start : start + size, :cut], NT)[0:1]
    sums = []
    for first in range(start, start + size, LANES):
        parts = []
        for sub in range(first, first + LANES, 64):
            total = None
            for column in range(cut, columns, LANES):
                term = feat_ref[sub : sub + 64, column : column + LANES].astype(F32) * weight[
                    0:1, column : column + LANES
                ]
                total = term if total is None else total + term
            parts.append(total)
        sums.append(jnp.sum(jnp.concatenate(parts, axis=0).T, axis=0, keepdims=True))
    return matrix + jnp.concatenate(sums, axis=1)


def front_kernel(
    ids_hbm,
    table_hbm,
    weight_hbm,
    feat_hbm,
    packet_ref,
    feat_ref,
    route_ref,
    ids_ref,
    table_ref,
    weight_ref,
    small_sems,
    feat_sems,
    *,
    mem_dev,
    chunks,
):
    rows = ids_ref.shape[1]
    small = [
        pltpu.make_async_copy(source, target, small_sems.at[i])
        for i, (source, target) in enumerate(
            ((ids_hbm, ids_ref), (table_hbm, table_ref), (weight_hbm, weight_ref))
        )
    ]
    copies = []
    start = 0
    for i, size in enumerate(chunks):
        here = pl.ds(start, size)
        copies.append(pltpu.make_async_copy(feat_hbm.at[here], feat_ref.at[here], feat_sems.at[i]))
        start += size
    for copy in small + copies:
        copy.start()
    for copy in small:
        copy.wait()

    ids = ids_ref[...]
    table = table_ref[...]
    owner_table = (table // mem_dev).astype(F32).astype(BF16)
    slot_table = (table % mem_dev).astype(F32).astype(BF16)
    both = jnp.concatenate([owner_table, slot_table], axis=1)
    found = dot(both, hot_rows(table.shape[0], ids // LANES), TN)
    low_hot = sublane_iota((LANES, rows)) == ids % LANES
    owner = jnp.sum(jnp.where(low_hot, found[:LANES], 0.0), axis=0, keepdims=True)
    slot = jnp.sum(jnp.where(low_hot, found[LANES:], 0.0), axis=0, keepdims=True)
    owner_hot = sublane_iota((LANES, rows)) == owner.astype(jnp.int32)
    hot = jnp.where(owner_hot, 1.0, 0.0).astype(BF16)
    earlier = jnp.where(sublane_iota((rows, rows)) < lane_iota((rows, rows)), 1.0, 0.0).astype(BF16)
    before = dot(hot, earlier, NN)
    rank = jnp.sum(jnp.where(owner_hot, before, 0.0), axis=0, keepdims=True)
    route_ref[0:1, :] = owner
    route_ref[1:2, :] = rank
    route_ref[2:3, :] = slot

    packet_ref[:, feat_ref.shape[0] :] = owner * CAPACITY + rank
    weight = jnp.broadcast_to(weight_ref[...].astype(BF16).astype(F32), (8, weight_ref.shape[1]))
    start = 0
    for copy, size in zip(copies, chunks):
        copy.wait()
        for first in range(start, start + size, 512):
            packet_ref[:, first : first + 512] = margin_chunk(weight, feat_ref, first, 512)
        start += size


def front(ids, table, weight, features, mem_dev):
    rows = ids.shape[1]
    examples, columns = features.shape
    chunks = (examples // 2, examples // 2)
    arguments = (ids, table, weight, features)
    return pl.pallas_call(
        functools.partial(front_kernel, mem_dev=mem_dev, chunks=chunks),
        in_specs=[pl.BlockSpec(memory_space=pl.ANY)] * 4,
        out_specs=[VMEM_SPEC] * 3,
        out_shape=[
            jax.ShapeDtypeStruct((1, examples + rows), F32),
            pltpu.VMEM((examples, columns), BF16),
            pltpu.VMEM((8, rows), F32),
        ],
        scratch_shapes=[
            pltpu.VMEM(ids.shape, jnp.int32),
            pltpu.VMEM(table.shape, jnp.int32),
            pltpu.VMEM(weight.shape, F32),
            pltpu.SemaphoreType.DMA((3,)),
            pltpu.SemaphoreType.DMA((len(chunks),)),
        ],
        compiler_params=vmem(16),
        name="front",
    )(*(pltpu.with_memory_space_constraint(argument, pltpu.HBM) for argument in arguments))


def place_kernel(route_ref, labels_ref, rows_ref, buf_ref, meta_ref):
    rows, width = rows_ref.shape
    owner = route_ref[0:1, :].astype(jnp.int32)
    rank = route_ref[1:2, :].astype(jnp.int32)
    slot = route_ref[2:3, :]
    first = pl.multiple_of(lax.axis_index("feat") * rows, rows)
    labels = labels_ref[:, pl.ds(first, rows)].astype(F32)
    owner_hot = hot_rows(LANES, owner)
    high, low = split(rows_ref[...])
    parts = jnp.concatenate([high, low], axis=1)
    group = 8
    for base in range(0, CAPACITY, group):
        place = [owner_hot * jnp.where(rank == base + i, 1.0, 0.0).astype(BF16) for i in range(group)]
        moved = dot(jnp.concatenate(place, axis=0), parts, NN)
        moved = moved[:, :width] + moved[:, width:]
        for i in range(group):
            here = slice(i * LANES, (i + 1) * LANES)
            buf_ref[per_owner(LEFT + base + i), :] = moved[here, :LANES]
            buf_ref[per_owner(RIGHT + base + i), :] = moved[here, LANES:]
    buf_ref[per_owner(SIDE), :] = jnp.zeros((LANES, LANES), F32)
    slot_hot = owner_hot * slot.astype(BF16)
    label_hot = owner_hot * labels.astype(BF16)
    meta_ref[...] = dot(slot_hot, hot_rows(LANES, rank + 4 * CAPACITY), NT) + dot(
        label_hot, hot_rows(LANES, rank + 5 * CAPACITY), NT
    )


def place(routes, labels, member_rows):
    buf = (LANES * MESSAGE, LANES)
    return pl.pallas_call(
        place_kernel,
        in_specs=[VMEM_SPEC] * 3,
        out_specs=[VMEM_SPEC] * 2,
        out_shape=[pltpu.VMEM(buf, F32), jax.ShapeDtypeStruct((LANES, LANES), F32)],
        compiler_params=vmem(16),
        name="place",
    )(routes, labels, member_rows)


def to_row(table):
    return jnp.concatenate([table[i : i + 1, :] for i in range(table.shape[0])], axis=1)


def to_table(row):
    return jnp.concatenate([row[:, i : i + LANES] for i in range(0, row.shape[1], LANES)], axis=0)


def grad_kernel(
    p0,
    p1,
    p2,
    p3,
    offset_ref,
    labels_ref,
    feat_ref,
    meta_ref,
    copies_ref,
    owner_ref,
    lane_ref,
):
    count = offset_ref.shape[1]
    block = p0.shape[1] - count
    for hop, packet_ref in enumerate((p0, p1, p2, p3)):
        number = lax.rem(lax.axis_index("feat") - hop + 4, 4)
        target = packet_ref[:, count:].astype(jnp.int32)
        here = pl.ds(pl.multiple_of(number * block, block), block)
        owner_ref[:, here] = hot_rows(LANES, target // CAPACITY)
        lane_ref[:, here] = hot_rows(LANES, number * CAPACITY + target % CAPACITY)
    margin = (p0[:, :count] + p2[:, :count]) + (p1[:, :count] + p3[:, :count]) + offset_ref[...]
    residual = (jax.nn.sigmoid(margin) - labels_ref[...].astype(F32)).astype(BF16)
    grad = dot(jnp.broadcast_to(residual, (8, count)), feat_ref[...], NN)[0:1]
    copies_ref[...] = jnp.broadcast_to(to_table(grad)[None], copies_ref.shape)


def grad_pass(packets, offset, labels, features, meta, peers):
    examples, columns = features.shape
    shape = (peers, columns // LANES, LANES)
    return pl.pallas_call(
        grad_kernel,
        in_specs=[VMEM_SPEC] * 7 + [pl.BlockSpec(memory_space=pl.ANY)],
        out_specs=[VMEM_SPEC] * 3,
        out_shape=[pltpu.VMEM(shape, F32)] + [pltpu.VMEM((LANES, examples), BF16)] * 2,
        compiler_params=vmem(16),
        name="grad",
    )(
        *packets,
        offset,
        labels,
        pltpu.with_memory_space_constraint(features, pltpu.VMEM),
        meta,
    )


def new_kernel(
    grads_ref,
    weight_ref,
    meta_ref,
    owner_ref,
    lane_ref,
    feat_ref,
    buf_ref,
    updated_hbm,
    send_ref,
    updated_ref,
    sem,
    *,
    examples,
):
    gradient = to_row(jnp.sum(grads_ref[...], axis=0)) / examples + RIDGE_FIXED * weight_ref[...]
    updated = weight_ref[...] - STEP_FIXED * gradient
    updated_ref[...] = updated
    result = pltpu.make_async_copy(updated_ref, updated_hbm, sem)
    result.start()
    weight = jnp.broadcast_to(updated.astype(BF16).astype(F32), (8, updated.shape[1]))
    count = feat_ref.shape[0]
    size = 512
    send = meta_ref[...]
    for start in range(0, count, size):
        here = slice(start, start + size)
        high, low = split(margin_chunk(weight, feat_ref, start, size))
        owner_hot = owner_ref[:, here]
        both = dot(jnp.concatenate([owner_hot * high, owner_hot * low], axis=0), lane_ref[:, here], NT)
        send = send + both[:LANES] + both[LANES:]
    send_ref[per_owner(SIDE), :] = send
    result.wait()


def new_pass(grads, weight, meta, owner_hot, lane_hot, features, row_buf, examples):
    columns = features.shape[1]
    return pl.pallas_call(
        functools.partial(new_kernel, examples=examples),
        in_specs=[VMEM_SPEC] * 7,
        out_specs=[pl.BlockSpec(memory_space=pltpu.HBM), VMEM_SPEC],
        out_shape=[pltpu.HBM((1, columns), F32), pltpu.VMEM(row_buf.shape, F32)],
        input_output_aliases={6: 1},
        scratch_shapes=[pltpu.VMEM((1, columns), F32), pltpu.SemaphoreType.DMA],
        compiler_params=vmem(16),
        name="new",
    )(
        grads,
        weight,
        meta,
        owner_hot,
        lane_hot,
        pltpu.with_memory_space_constraint(features, pltpu.VMEM),
        pltpu.with_memory_space_constraint(row_buf, pltpu.VMEM),
    )


def members_kernel(
    recv_ref,
    params_ref,
    counts_ref,
    route_hbm,
    out_ref,
    back_ref,
    route_ref,
    high_ref,
    low_ref,
    across_high_ref,
    across_low_ref,
    sem,
):
    keep = pltpu.make_async_copy(route_hbm, route_ref, sem)
    keep.start()
    old = params_ref[...]
    old_scores = []
    for k in range(0, CAPACITY, 2):
        rows = jnp.concatenate(
            [
                jnp.concatenate([recv_ref[per_owner(LEFT + i), :], recv_ref[per_owner(RIGHT + i), :]], axis=1)
                for i in (k, k + 1)
            ],
            axis=0,
        )
        here = pl.ds(k * LANES, 2 * LANES)
        high, low = split(rows)
        high_ref[here, :], low_ref[here, :] = high, low
        high, low = split(rows.T)
        across_high_ref[:, here], across_low_ref[:, here] = high, low
        old_scores.append(dot_split(old, high, low, NN))
    side = recv_ref[per_owner(SIDE), :].T
    groups = lax.axis_size("feat")
    lane = lane_iota((CAPACITY, LANES))
    offsets = jnp.zeros((CAPACITY, LANES), F32)
    for block in range(groups):
        part = side[block * CAPACITY : (block + 1) * CAPACITY]
        whole = part
        for hop in range(1, groups):
            whole = whole + pltpu.roll(part, hop, 1)
        whole = pltpu.roll(whole, (block - groups + 1) % LANES, 1)
        offsets = jnp.where(lane % groups == block, whole, offsets)
    offset = to_row(offsets)
    slot = to_row(side[4 * CAPACITY : 5 * CAPACITY]).astype(jnp.int32)
    label = to_row(side[5 * CAPACITY : 6 * CAPACITY])
    members = params_ref.shape[0]
    mask = sublane_iota((members, slot.shape[1])) == slot

    def own(value):
        return jnp.sum(jnp.where(mask, value, 0.0), axis=0, keepdims=True)

    high, low = high_ref[...], low_ref[...]
    across_high, across_low = across_high_ref[...], across_low_ref[...]
    diagonal = sublane_iota((members, members)) == lane_iota((members, members))
    scales = jnp.broadcast_to(1.0 / (counts_ref[...].astype(F32) + 1.0), (members, members))
    scaling = jnp.sum(jnp.where(diagonal, scales, 0.0), axis=1, keepdims=True)
    margin = offset + own(jnp.concatenate(old_scores, axis=1))
    probability = jax.nn.sigmoid(margin)
    weight = probability * (1.0 - probability)
    errors = jnp.where(mask, label - probability, 0.0)
    remains = scaling * dot_split(errors, high, low, NN) - RIDGE_MEMBER * old
    direction = remains
    delta = jnp.zeros_like(remains)
    norm_now = jnp.sum(remains * remains, axis=1, keepdims=True)
    for step in range(CG_STEPS):
        along = jnp.where(mask, dot_split(direction, across_high, None if step == 2 else across_low, NN), 0.0)
        weighted = along * weight
        curve = scaling * jnp.sum(weighted * along, axis=1, keepdims=True) + RIDGE_MEMBER * jnp.sum(
            direction * direction, axis=1, keepdims=True
        )
        step_size = norm_now / (curve + TINY)
        delta = delta + step_size * direction
        margin = margin + jnp.sum(along * step_size, axis=0, keepdims=True)
        if step < CG_STEPS - 1:
            image = scaling * dot_split(weighted, high, None if step == 1 else low, NN) + RIDGE_MEMBER * direction
            remains = remains - step_size * image
            norm_next = jnp.sum(remains * remains, axis=1, keepdims=True)
            direction = remains + (norm_next / (norm_now + TINY)) * direction
            norm_now = norm_next
    out_ref[...] = old + delta
    table = jnp.concatenate(
        [margin[:, k * LANES : (k + 1) * LANES] for k in range(CAPACITY)]
        + [jnp.zeros((LANES - CAPACITY, LANES), F32)],
        axis=0,
    )
    back_ref[...] = table.T
    keep.wait()


def members_pass(recv, member_params, counts, routes):
    members, width = member_params.shape
    slots = LANES * CAPACITY
    held, across = pltpu.VMEM((slots, width), BF16), pltpu.VMEM((width, slots), BF16)
    return pl.pallas_call(
        members_kernel,
        in_specs=[VMEM_SPEC] * 3 + [pl.BlockSpec(memory_space=pl.ANY)],
        out_specs=[VMEM_SPEC] * 3,
        out_shape=[
            pltpu.VMEM(member_params.shape, F32),
            jax.ShapeDtypeStruct((LANES, LANES), F32),
            pltpu.VMEM(routes.shape, F32),
        ],
        scratch_shapes=[held, held, across, across, pltpu.SemaphoreType.DMA],
        compiler_params=vmem(16),
        name="members",
    )(recv, member_params, counts, routes)


def collect_kernel(back_ref, route_ref, params_ref, out_hbm, params_hbm, out_ref, sems):
    result = pltpu.make_async_copy(params_ref, params_hbm, sems.at[0])
    result.start()
    high, low = split(back_ref[:, :CAPACITY])
    hot = hot_rows(LANES, route_ref[0:1, :].astype(jnp.int32))
    found = dot(jnp.concatenate([high, low], axis=0), jnp.concatenate([hot, hot], axis=0), TN)
    here = sublane_iota(found.shape) == route_ref[1:2, :].astype(jnp.int32)
    out_ref[...] = jnp.sum(jnp.where(here, found, 0.0), axis=0, keepdims=True)
    out = pltpu.make_async_copy(out_ref, out_hbm, sems.at[1])
    out.start()
    result.wait()
    out.wait()


def collect(back, routes, updated_params):
    return pl.pallas_call(
        collect_kernel,
        in_specs=[VMEM_SPEC] * 3,
        out_specs=[pl.BlockSpec(memory_space=pltpu.HBM)] * 2,
        out_shape=[pltpu.HBM((1, routes.shape[1]), F32), pltpu.HBM(updated_params.shape, F32)],
        scratch_shapes=[pltpu.VMEM((1, routes.shape[1]), F32), pltpu.SemaphoreType.DMA((2,))],
        compiler_params=vmem(8),
        name="collect",
    )(back, routes, pltpu.with_memory_space_constraint(updated_params, pltpu.VMEM))


def behind(value, axis):
    size = lax.axis_size(axis)
    return [value] + [
        lax.ppermute(value, axis, [(i, (i + hop) % size) for i in range(size)])
        for hop in range(1, size)
    ]


def gather(copies, axes):
    return lax.all_to_all(copies, axes, split_axis=0, concat_axis=0, tiled=True)


def exchange(table):
    sent = table.reshape(LANES, 1, -1)
    got = lax.all_to_all(sent, ALL, split_axis=0, concat_axis=0, tiled=True)
    return got.reshape(table.shape)


def body(
    features,
    fixed_weight,
    prior_offset,
    labels,
    impression_member,
    member_position,
    member_counts,
    member_features,
    member_params,
):
    owners = lax.axis_size(ALL)
    mem_dev = member_params.shape[0]
    examples = features.shape[0] * owners // lax.axis_size("feat")
    weight = fixed_weight[None]
    label_row = labels[None]

    packet, held, routes = front(
        impression_member[None],
        member_position.reshape(-1, LANES),
        weight,
        features,
        mem_dev,
    )
    packets = behind(packet, "feat")
    row_buf, meta = place(routes, label_row, member_features)
    dp = ("z", "y", "core")
    grad, owner_hot, lane_hot = grad_pass(
        packets, prior_offset[None], label_row, held, meta, lax.axis_size(dp)
    )
    grads = gather(grad, dp)
    updated, send = new_pass(grads, weight, meta, owner_hot, lane_hot, held, row_buf, examples)
    updated_params, back, routes = members_pass(
        exchange(send), member_params, member_counts[None], routes
    )
    total, updated_params = collect(exchange(back), routes, updated_params)
    return updated[0], updated_params, total[0]


def solution(mesh):
    split_mesh = Mesh(mesh.devices.reshape(4, 4, 2, 4), ALL)
    dp = ("z", "y", "core")
    placed = (
        P(dp, "feat"),
        P("feat"),
        P(dp),
        P(dp),
        P(ALL),
        P(),
        P(ALL),
        P(ALL, None),
        P(ALL, None),
    )
    return jax.shard_map(
        body,
        mesh=split_mesh,
        in_specs=placed,
        out_specs=(P("feat"), P(ALL, None), P(ALL)),
        check_vma=False,
    )
```

```python
import functools

import jax
import jax.numpy as jnp
from jax import lax
from jax.experimental import pallas as pl
from jax.experimental.pallas import tpu as pltpu
from jax.sharding import Mesh
from jax.sharding import PartitionSpec as P

RIDGE_FIXED = 0.1
STEP_FIXED = 2.0
RIDGE_MEMBER = 0.25
TINY = 1e-30
CG_STEPS = 3
F32 = jnp.float32
BF16 = jnp.bfloat16
LANES = 128
CAPACITY = 16
LEFT, RIGHT, SIDE, MESSAGE = 0, CAPACITY, 2 * CAPACITY, 2 * CAPACITY + 1
ALL = ("z", "y", "core", "feat")
BACK = ("core", "z", "y", "feat")
NN = (((1,), (0,)), ((), ()))
NT = (((1,), (1,)), ((), ()))
TN = (((0,), (0,)), ((), ()))
VMEM_SPEC = pl.BlockSpec(memory_space=pltpu.VMEM)


def dot(left, right, dims):
    return lax.dot_general(left, right, dims, preferred_element_type=F32)


def split(value):
    high = value.astype(BF16)
    return high, (value - high.astype(F32)).astype(BF16)


def dot_split(left, high, low, dims):
    left_high, left_low = split(left)
    rows = left.shape[0]
    both = dot(jnp.concatenate([left_high, left_low], axis=0), high, dims)
    total = both[:rows] + both[rows:]
    return total if low is None else total + dot(left_high, low, dims)


def sublane_iota(shape):
    return lax.broadcasted_iota(jnp.int32, shape, 0)


def lane_iota(shape):
    return lax.broadcasted_iota(jnp.int32, shape, 1)


def hot_rows(count, index):
    number = sublane_iota((count, LANES)).astype(F32).astype(BF16)
    index = index.astype(F32).astype(BF16)
    one, zero = jnp.ones((), BF16), jnp.zeros((), BF16)
    return jnp.concatenate(
        [
            jnp.where(number == index[:, start : start + LANES], one, zero)
            for start in range(0, index.shape[1], LANES)
        ],
        axis=1,
    )


def per_owner(row):
    return pl.ds(row, LANES, stride=MESSAGE)


def vmem(vmem_mib):
    return pltpu.CompilerParams(vmem_limit_bytes=vmem_mib << 20)


def margin_chunk(weight, feat_ref, start, size):
    columns = feat_ref.shape[1]
    cut = columns // 2
    matrix = dot(weight[:, :cut].astype(BF16), feat_ref[start : start + size, :cut], NT)[0:1]
    sums = []
    for first in range(start, start + size, LANES):
        parts = []
        for sub in range(first, first + LANES, 64):
            total = None
            for column in range(cut, columns, LANES):
                term = feat_ref[sub : sub + 64, column : column + LANES].astype(F32) * weight[
                    0:1, column : column + LANES
                ]
                total = term if total is None else total + term
            parts.append(total)
        sums.append(jnp.sum(jnp.concatenate(parts, axis=0).T, axis=0, keepdims=True))
    return matrix + jnp.concatenate(sums, axis=1)


def front_kernel(
    ids_hbm,
    table_hbm,
    weight_hbm,
    feat_hbm,
    packet_ref,
    feat_ref,
    route_ref,
    ids_ref,
    table_ref,
    weight_ref,
    small_sems,
    feat_sems,
    *,
    mem_dev,
    chunks,
):
    rows = ids_ref.shape[1]
    small = [
        pltpu.make_async_copy(source, target, small_sems.at[i])
        for i, (source, target) in enumerate(
            ((ids_hbm, ids_ref), (table_hbm, table_ref), (weight_hbm, weight_ref))
        )
    ]
    copies = []
    start = 0
    for i, size in enumerate(chunks):
        here = pl.ds(start, size)
        copies.append(pltpu.make_async_copy(feat_hbm.at[here], feat_ref.at[here], feat_sems.at[i]))
        start += size
    for copy in small + copies:
        copy.start()
    for copy in small:
        copy.wait()

    ids = ids_ref[...]
    table = table_ref[...]
    owner_table = (table // mem_dev).astype(F32).astype(BF16)
    slot_table = (table % mem_dev).astype(F32).astype(BF16)
    both = jnp.concatenate([owner_table, slot_table], axis=1)
    found = dot(both, hot_rows(table.shape[0], ids // LANES), TN)
    low_hot = sublane_iota((LANES, rows)) == ids % LANES
    owner = jnp.sum(jnp.where(low_hot, found[:LANES], 0.0), axis=0, keepdims=True)
    slot = jnp.sum(jnp.where(low_hot, found[LANES:], 0.0), axis=0, keepdims=True)
    owner_hot = sublane_iota((LANES, rows)) == owner.astype(jnp.int32)
    hot = jnp.where(owner_hot, 1.0, 0.0).astype(BF16)
    earlier = jnp.where(sublane_iota((rows, rows)) < lane_iota((rows, rows)), 1.0, 0.0).astype(BF16)
    before = dot(hot, earlier, NN)
    rank = jnp.sum(jnp.where(owner_hot, before, 0.0), axis=0, keepdims=True)
    route_ref[0:1, :] = owner
    route_ref[1:2, :] = rank
    route_ref[2:3, :] = slot

    packet_ref[:, feat_ref.shape[0] :] = owner * CAPACITY + rank
    weight = jnp.broadcast_to(weight_ref[...].astype(BF16).astype(F32), (8, weight_ref.shape[1]))
    start = 0
    for copy, size in zip(copies, chunks):
        copy.wait()
        for first in range(start, start + size, 512):
            packet_ref[:, first : first + 512] = margin_chunk(weight, feat_ref, first, 512)
        start += size


def front(ids, table, weight, features, mem_dev):
    rows = ids.shape[1]
    examples, columns = features.shape
    chunks = (examples // 2, examples // 2)
    arguments = (ids, table, weight, features)
    return pl.pallas_call(
        functools.partial(front_kernel, mem_dev=mem_dev, chunks=chunks),
        in_specs=[pl.BlockSpec(memory_space=pl.ANY)] * 4,
        out_specs=[VMEM_SPEC] * 3,
        out_shape=[
            jax.ShapeDtypeStruct((1, examples + rows), F32),
            pltpu.VMEM((examples, columns), BF16),
            pltpu.VMEM((8, rows), F32),
        ],
        scratch_shapes=[
            pltpu.VMEM(ids.shape, jnp.int32),
            pltpu.VMEM(table.shape, jnp.int32),
            pltpu.VMEM(weight.shape, F32),
            pltpu.SemaphoreType.DMA((3,)),
            pltpu.SemaphoreType.DMA((len(chunks),)),
        ],
        compiler_params=vmem(16),
        name="front",
    )(*(pltpu.with_memory_space_constraint(argument, pltpu.HBM) for argument in arguments))


def place_kernel(route_ref, labels_ref, rows_ref, buf_ref, meta_ref):
    rows, width = rows_ref.shape
    owner = route_ref[0:1, :].astype(jnp.int32)
    rank = route_ref[1:2, :].astype(jnp.int32)
    slot = route_ref[2:3, :]
    first = pl.multiple_of(lax.axis_index("feat") * rows, rows)
    labels = labels_ref[:, pl.ds(first, rows)].astype(F32)
    owner_hot = hot_rows(LANES, owner)
    high, low = split(rows_ref[...])
    parts = jnp.concatenate([high, low], axis=1)
    group = 8
    for base in range(0, CAPACITY, group):
        place = [owner_hot * jnp.where(rank == base + i, 1.0, 0.0).astype(BF16) for i in range(group)]
        moved = dot(jnp.concatenate(place, axis=0), parts, NN)
        moved = moved[:, :width] + moved[:, width:]
        for i in range(group):
            here = slice(i * LANES, (i + 1) * LANES)
            buf_ref[per_owner(LEFT + base + i), :] = moved[here, :LANES]
            buf_ref[per_owner(RIGHT + base + i), :] = moved[here, LANES:]
    buf_ref[per_owner(SIDE), :] = jnp.zeros((LANES, LANES), F32)
    slot_hot = owner_hot * slot.astype(BF16)
    label_hot = owner_hot * labels.astype(BF16)
    meta_ref[...] = dot(slot_hot, hot_rows(LANES, rank + 4 * CAPACITY), NT) + dot(
        label_hot, hot_rows(LANES, rank + 5 * CAPACITY), NT
    )


def place(routes, labels, member_rows):
    buf = (LANES * MESSAGE, LANES)
    return pl.pallas_call(
        place_kernel,
        in_specs=[VMEM_SPEC] * 3,
        out_specs=[VMEM_SPEC] * 2,
        out_shape=[pltpu.VMEM(buf, F32), jax.ShapeDtypeStruct((LANES, LANES), F32)],
        compiler_params=vmem(16),
        name="place",
    )(routes, labels, member_rows)


def to_row(table):
    return jnp.concatenate([table[i : i + 1, :] for i in range(table.shape[0])], axis=1)


def to_table(row):
    return jnp.concatenate([row[:, i : i + LANES] for i in range(0, row.shape[1], LANES)], axis=0)


def grad_kernel(
    p0,
    p1,
    p2,
    p3,
    offset_ref,
    labels_ref,
    feat_ref,
    meta_ref,
    copies_ref,
    owner_ref,
    lane_ref,
):
    count = offset_ref.shape[1]
    block = p0.shape[1] - count
    for hop, packet_ref in enumerate((p0, p1, p2, p3)):
        number = lax.rem(lax.axis_index("feat") - hop + 4, 4)
        target = packet_ref[:, count:].astype(jnp.int32)
        here = pl.ds(pl.multiple_of(number * block, block), block)
        owner_ref[:, here] = hot_rows(LANES, target // CAPACITY)
        lane_ref[:, here] = hot_rows(LANES, number * CAPACITY + target % CAPACITY)
    margin = (p0[:, :count] + p2[:, :count]) + (p1[:, :count] + p3[:, :count]) + offset_ref[...]
    residual = (jax.nn.sigmoid(margin) - labels_ref[...].astype(F32)).astype(BF16)
    grad = dot(jnp.broadcast_to(residual, (8, count)), feat_ref[...], NN)[0:1]
    copies_ref[...] = jnp.broadcast_to(to_table(grad)[None], copies_ref.shape)


def grad_pass(packets, offset, labels, features, meta, peers):
    examples, columns = features.shape
    shape = (peers, columns // LANES, LANES)
    return pl.pallas_call(
        grad_kernel,
        in_specs=[VMEM_SPEC] * 7 + [pl.BlockSpec(memory_space=pl.ANY)],
        out_specs=[VMEM_SPEC] * 3,
        out_shape=[pltpu.VMEM(shape, F32)] + [pltpu.VMEM((LANES, examples), BF16)] * 2,
        compiler_params=vmem(16),
        name="grad",
    )(
        *packets,
        offset,
        labels,
        pltpu.with_memory_space_constraint(features, pltpu.VMEM),
        meta,
    )


def new_kernel(
    grads_ref,
    weight_ref,
    meta_ref,
    owner_ref,
    lane_ref,
    feat_ref,
    buf_ref,
    updated_hbm,
    send_ref,
    updated_ref,
    sem,
    *,
    examples,
):
    gradient = to_row(jnp.sum(grads_ref[...], axis=0)) / examples + RIDGE_FIXED * weight_ref[...]
    updated = weight_ref[...] - STEP_FIXED * gradient
    updated_ref[...] = updated
    result = pltpu.make_async_copy(updated_ref, updated_hbm, sem)
    result.start()
    weight = jnp.broadcast_to(updated.astype(BF16).astype(F32), (8, updated.shape[1]))
    count = feat_ref.shape[0]
    size = 512
    send = meta_ref[...]
    for start in range(0, count, size):
        here = slice(start, start + size)
        high, low = split(margin_chunk(weight, feat_ref, start, size))
        owner_hot = owner_ref[:, here]
        both = dot(jnp.concatenate([owner_hot * high, owner_hot * low], axis=0), lane_ref[:, here], NT)
        send = send + both[:LANES] + both[LANES:]
    send_ref[per_owner(SIDE), :] = send
    result.wait()


def new_pass(grads, weight, meta, owner_hot, lane_hot, features, row_buf, examples):
    columns = features.shape[1]
    return pl.pallas_call(
        functools.partial(new_kernel, examples=examples),
        in_specs=[VMEM_SPEC] * 7,
        out_specs=[pl.BlockSpec(memory_space=pltpu.HBM), VMEM_SPEC],
        out_shape=[pltpu.HBM((1, columns), F32), pltpu.VMEM(row_buf.shape, F32)],
        input_output_aliases={6: 1},
        scratch_shapes=[pltpu.VMEM((1, columns), F32), pltpu.SemaphoreType.DMA],
        compiler_params=vmem(16),
        name="new",
    )(
        grads,
        weight,
        meta,
        owner_hot,
        lane_hot,
        pltpu.with_memory_space_constraint(features, pltpu.VMEM),
        pltpu.with_memory_space_constraint(row_buf, pltpu.VMEM),
    )


def members_kernel(
    recv_ref,
    params_ref,
    counts_ref,
    route_hbm,
    out_ref,
    back_ref,
    route_ref,
    high_ref,
    low_ref,
    across_high_ref,
    across_low_ref,
    sem,
):
    keep = pltpu.make_async_copy(route_hbm, route_ref, sem)
    keep.start()
    old = params_ref[...]
    old_scores = []
    for k in range(0, CAPACITY, 2):
        rows = jnp.concatenate(
            [
                jnp.concatenate([recv_ref[per_owner(LEFT + i), :], recv_ref[per_owner(RIGHT + i), :]], axis=1)
                for i in (k, k + 1)
            ],
            axis=0,
        )
        here = pl.ds(k * LANES, 2 * LANES)
        high, low = split(rows)
        high_ref[here, :], low_ref[here, :] = high, low
        high, low = split(rows.T)
        across_high_ref[:, here], across_low_ref[:, here] = high, low
        old_scores.append(dot_split(old, high, low, NN))
    side = recv_ref[per_owner(SIDE), :].T
    groups = lax.axis_size("feat")
    lane = lane_iota((CAPACITY, LANES))
    offsets = jnp.zeros((CAPACITY, LANES), F32)
    for block in range(groups):
        part = side[block * CAPACITY : (block + 1) * CAPACITY]
        whole = part
        for hop in range(1, groups):
            whole = whole + pltpu.roll(part, hop, 1)
        whole = pltpu.roll(whole, (block - groups + 1) % LANES, 1)
        offsets = jnp.where(lane % groups == block, whole, offsets)
    offset = to_row(offsets)
    slot = to_row(side[4 * CAPACITY : 5 * CAPACITY]).astype(jnp.int32)
    label = to_row(side[5 * CAPACITY : 6 * CAPACITY])
    members = params_ref.shape[0]
    mask = sublane_iota((members, slot.shape[1])) == slot

    def own(value):
        return jnp.sum(jnp.where(mask, value, 0.0), axis=0, keepdims=True)

    high, low = high_ref[...], low_ref[...]
    across_high, across_low = across_high_ref[...], across_low_ref[...]
    diagonal = sublane_iota((members, members)) == lane_iota((members, members))
    scales = jnp.broadcast_to(1.0 / (counts_ref[...].astype(F32) + 1.0), (members, members))
    scaling = jnp.sum(jnp.where(diagonal, scales, 0.0), axis=1, keepdims=True)
    margin = offset + own(jnp.concatenate(old_scores, axis=1))
    probability = jax.nn.sigmoid(margin)
    weight = probability * (1.0 - probability)
    errors = jnp.where(mask, label - probability, 0.0)
    remains = scaling * dot_split(errors, high, low, NN) - RIDGE_MEMBER * old
    direction = remains
    delta = jnp.zeros_like(remains)
    norm_now = jnp.sum(remains * remains, axis=1, keepdims=True)
    for step in range(CG_STEPS):
        along = jnp.where(mask, dot_split(direction, across_high, None if step == 2 else across_low, NN), 0.0)
        weighted = along * weight
        curve = scaling * jnp.sum(weighted * along, axis=1, keepdims=True) + RIDGE_MEMBER * jnp.sum(
            direction * direction, axis=1, keepdims=True
        )
        step_size = norm_now / (curve + TINY)
        delta = delta + step_size * direction
        margin = margin + jnp.sum(along * step_size, axis=0, keepdims=True)
        if step < CG_STEPS - 1:
            image = scaling * dot_split(weighted, high, None if step == 1 else low, NN) + RIDGE_MEMBER * direction
            remains = remains - step_size * image
            norm_next = jnp.sum(remains * remains, axis=1, keepdims=True)
            direction = remains + (norm_next / (norm_now + TINY)) * direction
            norm_now = norm_next
    out_ref[...] = old + delta
    table = jnp.concatenate(
        [margin[:, k * LANES : (k + 1) * LANES] for k in range(CAPACITY)]
        + [jnp.zeros((LANES - CAPACITY, LANES), F32)],
        axis=0,
    )
    by_source = table.T
    cores, chip = lax.axis_size("core"), lax.axis_size("feat")
    for number in range(LANES // chip):
        core, place = number % cores, number // cores
        start = core * (LANES // cores) + place * chip
        back_ref[start : start + chip, :] = by_source[number * chip : (number + 1) * chip]
    keep.wait()


def members_pass(recv, member_params, counts, routes):
    members, width = member_params.shape
    slots = LANES * CAPACITY
    held, across = pltpu.VMEM((slots, width), BF16), pltpu.VMEM((width, slots), BF16)
    return pl.pallas_call(
        members_kernel,
        in_specs=[VMEM_SPEC] * 3 + [pl.BlockSpec(memory_space=pl.ANY)],
        out_specs=[VMEM_SPEC] * 3,
        out_shape=[
            pltpu.VMEM(member_params.shape, F32),
            jax.ShapeDtypeStruct((LANES, LANES), F32),
            pltpu.VMEM(routes.shape, F32),
        ],
        scratch_shapes=[held, held, across, across, pltpu.SemaphoreType.DMA],
        compiler_params=vmem(16),
        name="members",
    )(recv, member_params, counts, routes)


def collect_kernel(back_ref, route_ref, params_ref, out_hbm, params_hbm, out_ref, sems):
    result = pltpu.make_async_copy(params_ref, params_hbm, sems.at[0])
    result.start()
    high, low = split(back_ref[:, :CAPACITY])
    owner = route_ref[0:1, :].astype(jnp.int32)
    cores, chip = lax.axis_size("core"), lax.axis_size("feat")
    core, place = owner // chip % cores, owner // (chip * cores)
    hot = hot_rows(LANES, core * (LANES // cores) + place * chip + owner % chip)
    found = dot(jnp.concatenate([high, low], axis=0), jnp.concatenate([hot, hot], axis=0), TN)
    here = sublane_iota(found.shape) == route_ref[1:2, :].astype(jnp.int32)
    out_ref[...] = jnp.sum(jnp.where(here, found, 0.0), axis=0, keepdims=True)
    out = pltpu.make_async_copy(out_ref, out_hbm, sems.at[1])
    out.start()
    result.wait()
    out.wait()


def collect(back, routes, updated_params):
    return pl.pallas_call(
        collect_kernel,
        in_specs=[VMEM_SPEC] * 3,
        out_specs=[pl.BlockSpec(memory_space=pltpu.HBM)] * 2,
        out_shape=[pltpu.HBM((1, routes.shape[1]), F32), pltpu.HBM(updated_params.shape, F32)],
        scratch_shapes=[pltpu.VMEM((1, routes.shape[1]), F32), pltpu.SemaphoreType.DMA((2,))],
        compiler_params=vmem(8),
        name="collect",
    )(back, routes, pltpu.with_memory_space_constraint(updated_params, pltpu.VMEM))


def behind(value, axis):
    size = lax.axis_size(axis)
    return [value] + [
        lax.ppermute(value, axis, [(i, (i + hop) % size) for i in range(size)])
        for hop in range(1, size)
    ]


def gather(copies, axes):
    return lax.all_to_all(copies, axes, split_axis=0, concat_axis=0, tiled=True)


def exchange(table, axes):
    sent = table.reshape(LANES, 1, -1)
    got = lax.all_to_all(sent, axes, split_axis=0, concat_axis=0, tiled=True)
    return got.reshape(table.shape)


def body(
    features,
    fixed_weight,
    prior_offset,
    labels,
    impression_member,
    member_position,
    member_counts,
    member_features,
    member_params,
):
    owners = lax.axis_size(ALL)
    mem_dev = member_params.shape[0]
    examples = features.shape[0] * owners // lax.axis_size("feat")
    weight = fixed_weight[None]
    label_row = labels[None]

    packet, held, routes = front(
        impression_member[None],
        member_position.reshape(-1, LANES),
        weight,
        features,
        mem_dev,
    )
    packets = behind(packet, "feat")
    row_buf, meta = place(routes, label_row, member_features)
    dp = ("core", "z", "y")
    grad, owner_hot, lane_hot = grad_pass(
        packets, prior_offset[None], label_row, held, meta, lax.axis_size(dp)
    )
    grads = gather(grad, dp)
    updated, send = new_pass(grads, weight, meta, owner_hot, lane_hot, held, row_buf, examples)
    updated_params, back, routes = members_pass(
        exchange(send, ALL), member_params, member_counts[None], routes
    )
    total, updated_params = collect(exchange(back, BACK), routes, updated_params)
    return updated[0], updated_params, total[0]


def solution(mesh):
    split_mesh = Mesh(mesh.devices.reshape(4, 4, 2, 4), ALL)
    dp = ("z", "y", "core")
    placed = (
        P(dp, "feat"),
        P("feat"),
        P(dp),
        P(dp),
        P(ALL),
        P(),
        P(ALL),
        P(ALL, None),
        P(ALL, None),
    )
    return jax.shard_map(
        body,
        mesh=split_mesh,
        in_specs=placed,
        out_specs=(P("feat"), P(ALL, None), P(ALL)),
        check_vma=False,
    )
```

```python
import functools

import jax
import jax.numpy as jnp
from jax import lax
from jax.experimental import pallas as pl
from jax.experimental.pallas import tpu as pltpu
from jax.sharding import Mesh
from jax.sharding import PartitionSpec as P

RIDGE_FIXED = 0.1
STEP_FIXED = 2.0
RIDGE_MEMBER = 0.25
TINY = 1e-30
CG_STEPS = 3
F32 = jnp.float32
BF16 = jnp.bfloat16
LANES = 128
CAPACITY = 16
LEFT, RIGHT, SIDE, MESSAGE = 0, CAPACITY, 2 * CAPACITY, 2 * CAPACITY + 1
ALL = ("z", "y", "core", "feat")
BACK = ("core", "z", "y", "feat")
NN = (((1,), (0,)), ((), ()))
NT = (((1,), (1,)), ((), ()))
TN = (((0,), (0,)), ((), ()))
VMEM_SPEC = pl.BlockSpec(memory_space=pltpu.VMEM)


def dot(left, right, dims):
    return lax.dot_general(left, right, dims, preferred_element_type=F32)


def split(value):
    high = value.astype(BF16)
    return high, (value - high.astype(F32)).astype(BF16)


def dot_split(left, high, low, dims):
    left_high, left_low = split(left)
    rows = left.shape[0]
    both = dot(jnp.concatenate([left_high, left_low], axis=0), high, dims)
    total = both[:rows] + both[rows:]
    return total if low is None else total + dot(left_high, low, dims)


def sublane_iota(shape):
    return lax.broadcasted_iota(jnp.int32, shape, 0)


def lane_iota(shape):
    return lax.broadcasted_iota(jnp.int32, shape, 1)


def hot_rows(count, index):
    number = sublane_iota((count, LANES)).astype(F32).astype(BF16)
    index = index.astype(F32).astype(BF16)
    one, zero = jnp.ones((), BF16), jnp.zeros((), BF16)
    return jnp.concatenate(
        [
            jnp.where(number == index[:, start : start + LANES], one, zero)
            for start in range(0, index.shape[1], LANES)
        ],
        axis=1,
    )


def per_owner(row):
    return pl.ds(row, LANES, stride=MESSAGE)


def vmem(vmem_mib):
    return pltpu.CompilerParams(vmem_limit_bytes=vmem_mib << 20)


def margin_chunk(weight, feat_ref, start, size):
    columns = feat_ref.shape[1]
    cut = columns // 2
    matrix = dot(weight[:, :cut].astype(BF16), feat_ref[start : start + size, :cut], NT)[0:1]
    sums = []
    for first in range(start, start + size, LANES):
        parts = []
        for sub in range(first, first + LANES, 64):
            total = None
            for column in range(cut, columns, LANES):
                term = feat_ref[sub : sub + 64, column : column + LANES].astype(F32) * weight[
                    0:1, column : column + LANES
                ]
                total = term if total is None else total + term
            parts.append(total)
        sums.append(jnp.sum(jnp.concatenate(parts, axis=0).T, axis=0, keepdims=True))
    return matrix + jnp.concatenate(sums, axis=1)


def front_kernel(
    ids_hbm,
    table_hbm,
    weight_hbm,
    feat_hbm,
    packet_ref,
    feat_ref,
    route_ref,
    ids_ref,
    table_ref,
    weight_ref,
    small_sems,
    feat_sems,
    *,
    mem_dev,
    chunks,
):
    rows = ids_ref.shape[1]
    small = [
        pltpu.make_async_copy(source, target, small_sems.at[i])
        for i, (source, target) in enumerate(
            ((ids_hbm, ids_ref), (table_hbm, table_ref), (weight_hbm, weight_ref))
        )
    ]
    copies = []
    start = 0
    for i, size in enumerate(chunks):
        here = pl.ds(start, size)
        copies.append(pltpu.make_async_copy(feat_hbm.at[here], feat_ref.at[here], feat_sems.at[i]))
        start += size
    for copy in small + copies:
        copy.start()
    for copy in small:
        copy.wait()

    ids = ids_ref[...]
    table = table_ref[...]
    owner_table = (table // mem_dev).astype(F32).astype(BF16)
    slot_table = (table % mem_dev).astype(F32).astype(BF16)
    both = jnp.concatenate([owner_table, slot_table], axis=1)
    found = dot(both, hot_rows(table.shape[0], ids // LANES), TN)
    low_hot = sublane_iota((LANES, rows)) == ids % LANES
    owner = jnp.sum(jnp.where(low_hot, found[:LANES], 0.0), axis=0, keepdims=True)
    slot = jnp.sum(jnp.where(low_hot, found[LANES:], 0.0), axis=0, keepdims=True)
    owner_hot = sublane_iota((LANES, rows)) == owner.astype(jnp.int32)
    hot = jnp.where(owner_hot, 1.0, 0.0).astype(BF16)
    earlier = jnp.where(sublane_iota((rows, rows)) < lane_iota((rows, rows)), 1.0, 0.0).astype(BF16)
    before = dot(hot, earlier, NN)
    rank = jnp.sum(jnp.where(owner_hot, before, 0.0), axis=0, keepdims=True)
    route_ref[0:1, :] = owner
    route_ref[1:2, :] = rank
    route_ref[2:3, :] = slot

    packet_ref[:, feat_ref.shape[0] :] = owner * CAPACITY + rank
    weight = jnp.broadcast_to(weight_ref[...].astype(BF16).astype(F32), (8, weight_ref.shape[1]))
    start = 0
    for copy, size in zip(copies, chunks):
        copy.wait()
        for first in range(start, start + size, 512):
            packet_ref[:, first : first + 512] = margin_chunk(weight, feat_ref, first, 512)
        start += size


def front(ids, table, weight, features, mem_dev):
    rows = ids.shape[1]
    examples, columns = features.shape
    chunks = (examples // 2, examples // 2)
    arguments = (ids, table, weight, features)
    return pl.pallas_call(
        functools.partial(front_kernel, mem_dev=mem_dev, chunks=chunks),
        in_specs=[pl.BlockSpec(memory_space=pl.ANY)] * 4,
        out_specs=[VMEM_SPEC] * 3,
        out_shape=[
            jax.ShapeDtypeStruct((1, examples + rows), F32),
            pltpu.VMEM((examples, columns), BF16),
            pltpu.VMEM((8, rows), F32),
        ],
        scratch_shapes=[
            pltpu.VMEM(ids.shape, jnp.int32),
            pltpu.VMEM(table.shape, jnp.int32),
            pltpu.VMEM(weight.shape, F32),
            pltpu.SemaphoreType.DMA((3,)),
            pltpu.SemaphoreType.DMA((len(chunks),)),
        ],
        compiler_params=vmem(16),
        name="front",
    )(*(pltpu.with_memory_space_constraint(argument, pltpu.HBM) for argument in arguments))


def place_kernel(route_ref, labels_ref, rows_ref, buf_ref, meta_ref):
    rows, width = rows_ref.shape
    owner = route_ref[0:1, :].astype(jnp.int32)
    rank = route_ref[1:2, :].astype(jnp.int32)
    slot = route_ref[2:3, :]
    first = pl.multiple_of(lax.axis_index("feat") * rows, rows)
    labels = labels_ref[:, pl.ds(first, rows)].astype(F32)
    owner_hot = hot_rows(LANES, owner)
    high, low = split(rows_ref[...])
    parts = jnp.concatenate([high, low], axis=1)
    group = 8
    for base in range(0, CAPACITY, group):
        place = [owner_hot * jnp.where(rank == base + i, 1.0, 0.0).astype(BF16) for i in range(group)]
        moved = dot(jnp.concatenate(place, axis=0), parts, NN)
        moved = moved[:, :width] + moved[:, width:]
        for i in range(group):
            here = slice(i * LANES, (i + 1) * LANES)
            buf_ref[per_owner(LEFT + base + i), :] = moved[here, :LANES]
            buf_ref[per_owner(RIGHT + base + i), :] = moved[here, LANES:]
    buf_ref[per_owner(SIDE), :] = jnp.zeros((LANES, LANES), F32)
    slot_hot = owner_hot * slot.astype(BF16)
    label_hot = owner_hot * labels.astype(BF16)
    meta_ref[...] = dot(slot_hot, hot_rows(LANES, rank + 4 * CAPACITY), NT) + dot(
        label_hot, hot_rows(LANES, rank + 5 * CAPACITY), NT
    )


def place(routes, labels, member_rows):
    buf = (LANES * MESSAGE, LANES)
    return pl.pallas_call(
        place_kernel,
        in_specs=[VMEM_SPEC] * 3,
        out_specs=[VMEM_SPEC] * 2,
        out_shape=[pltpu.VMEM(buf, F32), jax.ShapeDtypeStruct((LANES, LANES), F32)],
        compiler_params=vmem(16),
        name="place",
    )(routes, labels, member_rows)


def to_row(table):
    return jnp.concatenate([table[i : i + 1, :] for i in range(table.shape[0])], axis=1)


def to_table(row):
    return jnp.concatenate([row[:, i : i + LANES] for i in range(0, row.shape[1], LANES)], axis=0)


def grad_kernel(
    p0,
    p1,
    p2,
    p3,
    offset_ref,
    labels_ref,
    feat_ref,
    meta_ref,
    copies_ref,
    owner_ref,
    lane_ref,
):
    count = offset_ref.shape[1]
    block = p0.shape[1] - count
    for hop, packet_ref in enumerate((p0, p1, p2, p3)):
        number = lax.rem(lax.axis_index("feat") - hop + 4, 4)
        target = packet_ref[:, count:].astype(jnp.int32)
        here = pl.ds(pl.multiple_of(number * block, block), block)
        owner_ref[:, here] = hot_rows(LANES, target // CAPACITY)
        lane_ref[:, here] = hot_rows(LANES, number * CAPACITY + target % CAPACITY)
    margin = (p0[:, :count] + p2[:, :count]) + (p1[:, :count] + p3[:, :count]) + offset_ref[...]
    residual = (jax.nn.sigmoid(margin) - labels_ref[...].astype(F32)).astype(BF16)
    grad = dot(jnp.broadcast_to(residual, (8, count)), feat_ref[...], NN)[0:1]
    copies_ref[...] = jnp.broadcast_to(to_table(grad)[None], copies_ref.shape)


def grad_pass(packets, offset, labels, features, meta, peers):
    examples, columns = features.shape
    shape = (peers, columns // LANES, LANES)
    return pl.pallas_call(
        grad_kernel,
        in_specs=[VMEM_SPEC] * 7 + [pl.BlockSpec(memory_space=pl.ANY)],
        out_specs=[VMEM_SPEC] * 3,
        out_shape=[pltpu.VMEM(shape, F32)] + [pltpu.VMEM((LANES, examples), BF16)] * 2,
        compiler_params=vmem(16),
        name="grad",
    )(
        *packets,
        offset,
        labels,
        pltpu.with_memory_space_constraint(features, pltpu.VMEM),
        meta,
    )


def new_kernel(
    grads_ref,
    weight_ref,
    meta_ref,
    owner_ref,
    lane_ref,
    feat_ref,
    buf_ref,
    updated_hbm,
    send_ref,
    updated_ref,
    sem,
    *,
    examples,
):
    gradient = to_row(jnp.sum(grads_ref[...], axis=0)) / examples + RIDGE_FIXED * weight_ref[...]
    updated = weight_ref[...] - STEP_FIXED * gradient
    updated_ref[...] = updated
    result = pltpu.make_async_copy(updated_ref, updated_hbm, sem)
    result.start()
    weight = jnp.broadcast_to(updated.astype(BF16).astype(F32), (8, updated.shape[1]))
    count = feat_ref.shape[0]
    size = 512
    send = meta_ref[...]
    for start in range(0, count, size):
        here = slice(start, start + size)
        high, low = split(margin_chunk(weight, feat_ref, start, size))
        owner_hot = owner_ref[:, here]
        both = dot(jnp.concatenate([owner_hot * high, owner_hot * low], axis=0), lane_ref[:, here], NT)
        send = send + both[:LANES] + both[LANES:]
    send_ref[per_owner(SIDE), :] = send
    result.wait()


def new_pass(grads, weight, meta, owner_hot, lane_hot, features, row_buf, examples):
    columns = features.shape[1]
    return pl.pallas_call(
        functools.partial(new_kernel, examples=examples),
        in_specs=[VMEM_SPEC] * 7,
        out_specs=[pl.BlockSpec(memory_space=pltpu.HBM), VMEM_SPEC],
        out_shape=[pltpu.HBM((1, columns), F32), pltpu.VMEM(row_buf.shape, F32)],
        input_output_aliases={6: 1},
        scratch_shapes=[pltpu.VMEM((1, columns), F32), pltpu.SemaphoreType.DMA],
        compiler_params=vmem(16),
        name="new",
    )(
        grads,
        weight,
        meta,
        owner_hot,
        lane_hot,
        pltpu.with_memory_space_constraint(features, pltpu.VMEM),
        pltpu.with_memory_space_constraint(row_buf, pltpu.VMEM),
    )


def members_kernel(
    recv_ref,
    params_ref,
    counts_ref,
    route_hbm,
    out_ref,
    back_ref,
    route_ref,
    high_ref,
    low_ref,
    across_high_ref,
    across_low_ref,
    sem,
):
    keep = pltpu.make_async_copy(route_hbm, route_ref, sem)
    keep.start()
    old = params_ref[...]
    old_scores = []
    for k in range(0, CAPACITY, 2):
        rows = jnp.concatenate(
            [
                jnp.concatenate([recv_ref[per_owner(LEFT + i), :], recv_ref[per_owner(RIGHT + i), :]], axis=1)
                for i in (k, k + 1)
            ],
            axis=0,
        )
        here = pl.ds(k * LANES, 2 * LANES)
        high, low = split(rows)
        high_ref[here, :], low_ref[here, :] = high, low
        high, low = split(rows.T)
        across_high_ref[:, here], across_low_ref[:, here] = high, low
        old_scores.append(dot_split(old, high, low, NN))
    side = recv_ref[per_owner(SIDE), :].T
    groups = lax.axis_size("feat")
    lane = lane_iota((CAPACITY, LANES))
    offsets = jnp.zeros((CAPACITY, LANES), F32)
    for block in range(groups):
        part = side[block * CAPACITY : (block + 1) * CAPACITY]
        whole = part
        for hop in range(1, groups):
            whole = whole + pltpu.roll(part, hop, 1)
        whole = pltpu.roll(whole, (block - groups + 1) % LANES, 1)
        offsets = jnp.where(lane % groups == block, whole, offsets)
    offset = to_row(offsets)
    slot = to_row(side[4 * CAPACITY : 5 * CAPACITY]).astype(jnp.int32)
    label = to_row(side[5 * CAPACITY : 6 * CAPACITY])
    members = params_ref.shape[0]
    mask = sublane_iota((members, slot.shape[1])) == slot

    def own(value):
        return jnp.sum(jnp.where(mask, value, 0.0), axis=0, keepdims=True)

    high, low = high_ref[...], low_ref[...]
    across_high, across_low = across_high_ref[...], across_low_ref[...]
    diagonal = sublane_iota((members, members)) == lane_iota((members, members))
    scales = jnp.broadcast_to(1.0 / (counts_ref[...].astype(F32) + 1.0), (members, members))
    scaling = jnp.sum(jnp.where(diagonal, scales, 0.0), axis=1, keepdims=True)
    margin = offset + own(jnp.concatenate(old_scores, axis=1))
    probability = jax.nn.sigmoid(margin)
    weight = probability * (1.0 - probability)
    errors = jnp.where(mask, label - probability, 0.0)
    remains = scaling * dot_split(errors, high, low, NN) - RIDGE_MEMBER * old
    direction = remains
    delta = jnp.zeros_like(remains)
    norm_now = jnp.sum(remains * remains, axis=1, keepdims=True)
    for step in range(CG_STEPS):
        along = jnp.where(mask, dot_split(direction, across_high, None if step == 2 else across_low, NN), 0.0)
        weighted = along * weight
        curve = scaling * jnp.sum(weighted * along, axis=1, keepdims=True) + RIDGE_MEMBER * jnp.sum(
            direction * direction, axis=1, keepdims=True
        )
        step_size = norm_now / (curve + TINY)
        delta = delta + step_size * direction
        margin = margin + jnp.sum(along * step_size, axis=0, keepdims=True)
        if step < CG_STEPS - 1:
            image = scaling * dot_split(weighted, high, None if step == 1 else low, NN) + RIDGE_MEMBER * direction
            remains = remains - step_size * image
            norm_next = jnp.sum(remains * remains, axis=1, keepdims=True)
            direction = remains + (norm_next / (norm_now + TINY)) * direction
            norm_now = norm_next
    out_ref[...] = old + delta
    table = jnp.concatenate(
        [margin[:, k * LANES : (k + 1) * LANES] for k in range(CAPACITY)]
        + [jnp.zeros((LANES - CAPACITY, LANES), F32)],
        axis=0,
    )
    by_source = table.T
    cores, chip = lax.axis_size("core"), lax.axis_size("feat")
    for number in range(LANES // chip):
        core, place = number % cores, number // cores
        start = core * (LANES // cores) + place * chip
        back_ref[start : start + chip, :] = by_source[number * chip : (number + 1) * chip]
    keep.wait()


def members_pass(recv, member_params, counts, routes):
    members, width = member_params.shape
    slots = LANES * CAPACITY
    held, across = pltpu.VMEM((slots, width), BF16), pltpu.VMEM((width, slots), BF16)
    return pl.pallas_call(
        members_kernel,
        in_specs=[VMEM_SPEC] * 3 + [pl.BlockSpec(memory_space=pl.ANY)],
        out_specs=[VMEM_SPEC] * 3,
        out_shape=[
            pltpu.VMEM(member_params.shape, F32),
            jax.ShapeDtypeStruct((LANES, LANES), F32),
            pltpu.VMEM(routes.shape, F32),
        ],
        scratch_shapes=[held, held, across, across, pltpu.SemaphoreType.DMA],
        compiler_params=vmem(16),
        name="members",
    )(recv, member_params, counts, routes)


def collect_kernel(back_ref, route_ref, params_ref, out_hbm, params_hbm, out_ref, sems):
    result = pltpu.make_async_copy(params_ref, params_hbm, sems.at[0])
    result.start()
    high, low = split(back_ref[:, :CAPACITY])
    owner = route_ref[0:1, :].astype(jnp.int32)
    cores, chip = lax.axis_size("core"), lax.axis_size("feat")
    core, place = owner // chip % cores, owner // (chip * cores)
    hot = hot_rows(LANES, core * (LANES // cores) + place * chip + owner % chip)
    found = dot(jnp.concatenate([high, low], axis=0), jnp.concatenate([hot, hot], axis=0), TN)
    here = sublane_iota(found.shape) == route_ref[1:2, :].astype(jnp.int32)
    out_ref[...] = jnp.sum(jnp.where(here, found, 0.0), axis=0, keepdims=True)
    out = pltpu.make_async_copy(out_ref, out_hbm, sems.at[1])
    out.start()
    result.wait()
    out.wait()


def collect(back, routes, updated_params):
    return pl.pallas_call(
        collect_kernel,
        in_specs=[VMEM_SPEC] * 3,
        out_specs=[pl.BlockSpec(memory_space=pltpu.HBM)] * 2,
        out_shape=[pltpu.HBM((1, routes.shape[1]), F32), pltpu.HBM(updated_params.shape, F32)],
        scratch_shapes=[pltpu.VMEM((1, routes.shape[1]), F32), pltpu.SemaphoreType.DMA((2,))],
        compiler_params=vmem(8),
        name="collect",
    )(back, routes, pltpu.with_memory_space_constraint(updated_params, pltpu.VMEM))


def behind(value, axis):
    size = lax.axis_size(axis)
    order = sorted(range(1, size), key=lambda hop: min(hop, size - hop))
    got = {hop: lax.ppermute(value, axis, [(i, (i + hop) % size) for i in range(size)]) for hop in order}
    return [value] + [got[hop] for hop in range(1, size)]


def gather(copies, axes):
    return lax.all_to_all(copies, axes, split_axis=0, concat_axis=0, tiled=True)


def exchange(table, axes):
    sent = table.reshape(LANES, 1, -1)
    got = lax.all_to_all(sent, axes, split_axis=0, concat_axis=0, tiled=True)
    return got.reshape(table.shape)


def body(
    features,
    fixed_weight,
    prior_offset,
    labels,
    impression_member,
    member_position,
    member_counts,
    member_features,
    member_params,
):
    owners = lax.axis_size(ALL)
    mem_dev = member_params.shape[0]
    examples = features.shape[0] * owners // lax.axis_size("feat")
    weight = fixed_weight[None]
    label_row = labels[None]

    packet, held, routes = front(
        impression_member[None],
        member_position.reshape(-1, LANES),
        weight,
        features,
        mem_dev,
    )
    packets = behind(packet, "feat")
    row_buf, meta = place(routes, label_row, member_features)
    dp = ("core", "z", "y")
    grad, owner_hot, lane_hot = grad_pass(
        packets, prior_offset[None], label_row, held, meta, lax.axis_size(dp)
    )
    grads = gather(grad, dp)
    updated, send = new_pass(grads, weight, meta, owner_hot, lane_hot, held, row_buf, examples)
    updated_params, back, routes = members_pass(
        exchange(send, ALL), member_params, member_counts[None], routes
    )
    total, updated_params = collect(exchange(back, BACK), routes, updated_params)
    return updated[0], updated_params, total[0]


def solution(mesh):
    split_mesh = Mesh(mesh.devices.reshape(4, 4, 2, 4), ALL)
    dp = ("z", "y", "core")
    placed = (
        P(dp, "feat"),
        P("feat"),
        P(dp),
        P(dp),
        P(ALL),
        P(),
        P(ALL),
        P(ALL, None),
        P(ALL, None),
    )
    return jax.shard_map(
        body,
        mesh=split_mesh,
        in_specs=placed,
        out_specs=(P("feat"), P(ALL, None), P(ALL)),
        check_vma=False,
    )
```
